512 devices in a mesh: seq: 64 (over y, z_lo, core), dp: 8 (over z_hi, x).
Axes of the slice: x: 4, y: 8, z: 8 (z_hi: 2, z_lo: 4; z = z_hi * 4 + z_lo), core: 2. Of those that a mesh axis runs over, the one named last changes fastest.
Arguments:
- query_rows: bfloat16 [8, 64, 256, 1024], P('dp', 'seq'), may hold values from -8 to 8
- key_rows: bfloat16 [8, 64, 256, 1024], P('dp', 'seq'), may hold values from -8 to 8
- value_rows: bfloat16 [8, 64, 256, 1024], P('dp', 'seq'), may hold values from -6 to 6
- upstream: bfloat16 [8, 64, 256, 1024], P('dp', 'seq'), may hold values from -6 to 6
- input_weights: bfloat16 [1024, 3072], P('seq'), may hold values from -0.1875 to 0.1875
- output_weight: bfloat16 [1024, 1024], P('seq'), may hold values from -0.1875 to 0.1875
Outputs:
- input_gradient: bfloat16 [8, 64, 256, 1024], P('dp', 'seq')
- weight_gradient: float32 [1024, 1024], P('seq')
The draws below stay inside these ranges and needn't reach their ends.
All inputs are finite; a program needn't handle non-finite values.
Results may differ from the reference program's by a relative error of at most 0.0067.
Values may be sent and summed in bfloat16 or wider, within the bound.
No kernel may reach another device: no remote copies, remote signals or barrier semaphores. Data moves between devices by JAX's collectives and lax.ppermute only.
A program may use at most 64 MiB of HBM per device.

```python
import math
import jax
import jax.numpy as jnp
from jax import lax

D = 1024
HEAD_DIM = 64
PATCHES = 256
CLIP_LEN = 32
GROUPS = 8
FRAMES_GROUP = 64
GROUP_TOKENS = 16384


def draw_query_rows(key, part):
    key = jax.random.fold_in(key, 7)
    result = jnp.clip(jax.random.normal(key, (GROUPS, FRAMES_GROUP, PATCHES, D), jnp.float32), -6.0, 6.0)
    return result.astype(jnp.bfloat16)


def draw_key_rows(key, part):
    key = jax.random.fold_in(key, 13)
    result = jnp.clip(jax.random.normal(key, (GROUPS, FRAMES_GROUP, PATCHES, D), jnp.float32), -6.0, 6.0)
    return result.astype(jnp.bfloat16)


def level_of(key, extent, shards, least, high):
    loudness = 1.0
    for axis_at, parts in shards:
        steps = jax.random.uniform(jax.random.fold_in(jax.random.fold_in(key, 6), axis_at), (parts,), jnp.float32, least / len(shards), high / len(shards))
        loudness = loudness * jnp.repeat(jnp.exp(steps), extent[axis_at] // parts).reshape((-1,) + (1,) * (len(extent) - 1 - axis_at))
    return loudness


def gaussian(key, dims, scale, reach, shards=(), kind=jnp.bfloat16):
    drawn = jax.random.normal(key, dims, jnp.float32) * scale
    if len(shards) > 0:
        drawn = level_of(key, dims, shards, -0.22, 0.18) * drawn
    return jnp.clip(drawn, min=-reach, max=reach).astype(kind)


def setup_inputs(seed: int = 0) -> dict:
    key_of = jax.random.split(jax.random.key(seed), 7)
    return {
        "query_rows": draw_query_rows(jax.random.fold_in(key_of[6], 71), 0),
        "key_rows": draw_key_rows(jax.random.fold_in(key_of[6], 71), 0),
        "value_rows": gaussian(key_of[2], (GROUPS, FRAMES_GROUP, PATCHES, D), 1.0, 6.0, ((0, 8), (1, 64))),
        "upstream": gaussian(key_of[3], (GROUPS, FRAMES_GROUP, PATCHES, D), 1.0, 6.0, ((0, 8), (1, 64))),
        "input_weights": gaussian(key_of[4], (D, 3 * D), D ** -0.5, 0.1875, ((0, 64),)),
        "output_weight": gaussian(key_of[5], (D, D), D ** -0.5, 0.1875, ((0, 64),)),
    }


def temporal_grads(query_group, key_group, value_group, context_grad):
    frame_count, patch_count, feature_width = query_group.shape
    head_count = feature_width // HEAD_DIM
    layout = (frame_count // CLIP_LEN, CLIP_LEN, patch_count, head_count, HEAD_DIM)
    score_scale = 1.0 / math.sqrt(HEAD_DIM)
    query_heads = query_group.reshape(layout).astype(jnp.float32)
    key_heads = key_group.reshape(layout).astype(jnp.float32)
    value_heads = value_group.reshape(layout).astype(jnp.float32)
    grad_heads = context_grad.reshape(layout).astype(jnp.float32)
    scores = jnp.einsum('ctphe,csphe->cphts', query_heads, key_heads) * score_scale
    attention = jax.nn.softmax(scores, axis=-1)
    attention_b = lax.optimization_barrier(attention.astype(jnp.bfloat16)).astype(jnp.float32)
    context = jnp.einsum('cphts,csphe->ctphe', attention_b, value_heads).astype(jnp.bfloat16)
    grad_scores = jnp.einsum('ctphe,csphe->cphts', grad_heads, value_heads)
    row_total = lax.optimization_barrier(jnp.sum(attention * grad_scores, axis=-1, keepdims=True))
    score_grad = attention * (grad_scores - row_total) * score_scale
    score_grad = lax.optimization_barrier(score_grad.astype(jnp.bfloat16)).astype(jnp.float32)
    grad_query = jnp.einsum('cphts,csphe->ctphe', score_grad, key_heads).astype(jnp.bfloat16)
    grad_key = jnp.einsum('cphts,ctphe->csphe', score_grad, query_heads).astype(jnp.bfloat16)
    grad_value = jnp.einsum('cphts,ctphe->csphe', attention_b, grad_heads).astype(jnp.bfloat16)
    shape_back = query_group.shape
    return (context.reshape(shape_back), grad_query.reshape(shape_back), grad_key.reshape(shape_back), grad_value.reshape(shape_back))

def reference(query_rows, key_rows, value_rows, upstream, input_weights, output_weight):
    factor = 1.0 / (GROUPS * math.sqrt(GROUP_TOKENS))

    def one_group(operands):
        query_group, key_group, value_group, grad_group = operands
        flat_grad = grad_group.reshape(-1, D)
        context_grad = jnp.dot(flat_grad, output_weight.T, preferred_element_type=jnp.float32)
        context_grad = context_grad.astype(jnp.bfloat16).reshape(grad_group.shape)
        context, grad_query, grad_key, grad_value = temporal_grads(query_group, key_group, value_group, context_grad)
        total = jnp.dot(grad_query.reshape(-1, D), input_weights[:, :D].T, preferred_element_type=jnp.float32)
        total = total + jnp.dot(grad_key.reshape(-1, D), input_weights[:, D:2 * D].T, preferred_element_type=jnp.float32)
        total = total + jnp.dot(grad_value.reshape(-1, D), input_weights[:, 2 * D:].T, preferred_element_type=jnp.float32)
        weight_term = jnp.dot(context.reshape(-1, D).T, flat_grad, preferred_element_type=jnp.float32)
        return (total.astype(jnp.bfloat16).reshape(grad_group.shape), weight_term)
    input_gradient, weight_terms = lax.map(one_group, (query_rows, key_rows, value_rows, upstream))
    return (input_gradient, lax.optimization_barrier(jnp.sum(weight_terms, axis=0)) * factor)
```

```python
import functools
import math

import jax
import jax.numpy as jnp
from jax import lax
from jax.experimental import pallas as pl
from jax.experimental.pallas import tpu as pltpu
from jax.sharding import Mesh
from jax.sharding import PartitionSpec as P

D = 1024
HEAD_DIM = 64
CLIP_LEN = 32
PATCH_BLOCK = 8
ROWS = CLIP_LEN * PATCH_BLOCK
PAIR = 2 * HEAD_DIM
SLICE = 256
CLIP_AXES = ("yl", "zl", "c")
Y_AXES = ("yh", "yl")
Z_AXES = ("zl", "zh")
NEG = -1e30


def ring(size, shift):
    return [(i, (i + shift) % size) for i in range(size)]


def z_ring(shift):
    def at(z):
        return (z % 4) * 2 + z // 4

    return [(at(z), at((z + shift) % 8)) for z in range(8)]


def dot(a, b, contract):
    return lax.dot_general(a, b, (contract, ((), ())), preferred_element_type=jnp.float32)


NN = ((1,), (0,))
NT = ((1,), (1,))
TN = ((0,), (0,))


def weight_rows(own, sibling, z_at, core, columns):
    parts = []
    for z_lo in range(4):
        step = lax.rem(z_lo - z_at + 4, 4)
        mine, other = own[step, 0][:, columns], sibling[step, 0][:, columns]
        first = core == 0
        parts.append(jnp.where(first, mine, other))
        parts.append(jnp.where(first, other, mine))
    return jnp.concatenate(parts, axis=0)


def attention_kernel(place, q_ref, k_ref, v_ref, u_ref, *refs):
    pieces, (g_ref, dw_ref, bias) = refs[:8], refs[8:]
    pair = pl.program_id(0)
    x_at, z_at, core = place[0], place[1], place[2]

    @pl.when(pair == 0)
    def _():
        row = lax.broadcasted_iota(jnp.int32, (ROWS, ROWS), 0)
        col = lax.broadcasted_iota(jnp.int32, (ROWS, ROWS), 1)
        bias[...] = jnp.where(lax.rem(row - col + ROWS, PATCH_BLOCK) == 0, 0.0, NEG)

    cg = jnp.zeros((ROWS, PAIR), jnp.float32)
    for d in range(4):
        w = weight_rows(pieces[d], pieces[4 + d], z_at, core, slice(None))
        at = pl.multiple_of(lax.rem(x_at + d, 4) * SLICE, SLICE)
        cg = cg + dot(u_ref[:, pl.ds(at, SLICE)], w, NT)
    cg = cg.astype(jnp.bfloat16)
    q, k, v = q_ref[...], k_ref[...], v_ref[...]
    first = lax.broadcasted_iota(jnp.int32, (ROWS, PAIR), 1) < HEAD_DIM
    zero = jnp.zeros((), jnp.bfloat16)
    context = grad_q = grad_k = grad_v = jnp.zeros((ROWS, PAIR), jnp.float32)
    for head in range(2):

        def only(a):
            return jnp.where(first, a, zero) if head == 0 else jnp.where(first, zero, a)

        q_h, k_h, v_h, cg_h = only(q), only(k), only(v), only(cg)
        scores = dot(q, k_h, NT) + bias[...]
        top = jnp.max(scores, axis=1, keepdims=True)
        e = jnp.exp2((scores - top) * (math.log2(math.e) / math.sqrt(HEAD_DIM)))
        attention = e * (1.0 / jnp.sum(e, axis=1, keepdims=True))
        attention_b = attention.astype(jnp.bfloat16)
        grad_scores = dot(cg, v_h, NT)
        total = jnp.sum(attention * grad_scores, axis=1, keepdims=True)
        score_grad = (attention * (grad_scores - total) * (1.0 / math.sqrt(HEAD_DIM))).astype(
            jnp.bfloat16
        )
        context = context + dot(attention_b, v_h, NN)
        grad_q = grad_q + dot(score_grad, k_h, NN)
        grad_k = grad_k + dot(score_grad, q_h, TN)
        grad_v = grad_v + dot(attention_b, cg_h, TN)
    for i, g in enumerate((grad_q, grad_k, grad_v)):
        at = pl.multiple_of(i * D + pair * PAIR, PAIR)
        g_ref[:, pl.ds(at, PAIR)] = g.astype(jnp.bfloat16)
    dw = dot(context.astype(jnp.bfloat16), u_ref[...], TN).astype(jnp.bfloat16)
    dw = dw.reshape(4, 2, 16, D)
    for c in range(2):
        rows = dw[:, c].reshape(64, D)
        for x in range(4):
            dw_ref[c, x, 0] = rows[:, x * SLICE : (x + 1) * SLICE]


def attention_call(place, moved, pieces):
    def column(base):
        return pl.BlockSpec((ROWS, PAIR), lambda i, s: (0, base + i))

    grid_spec = pltpu.PrefetchScalarGridSpec(
        num_scalar_prefetch=1,
        grid=(8,),
        in_specs=[
            column(0),
            column(8),
            column(16),
            pl.BlockSpec((ROWS, D), lambda i, s: (0, 3)),
        ]
        + [pl.BlockSpec((4, 1, 16, SLICE), lambda i, s: (0, i, 0, 3))] * 8,
        out_specs=[
            pl.BlockSpec((ROWS, 3 * D), lambda i, s: (0, 0)),
            pl.BlockSpec((2, 4, 1, 64, SLICE), lambda i, s: (0, 0, i, 0, 0)),
        ],
        scratch_shapes=[pltpu.VMEM((ROWS, ROWS), jnp.float32)],
    )
    return pl.pallas_call(
        attention_kernel,
        grid_spec=grid_spec,
        out_shape=[
            jax.ShapeDtypeStruct((ROWS, 3 * D), jnp.bfloat16),
            jax.ShapeDtypeStruct((2, 4, 8, 64, SLICE), jnp.bfloat16),
        ],
        compiler_params=pltpu.CompilerParams(vmem_limit_bytes=40 * 2**20),
        cost_estimate=pl.CostEstimate(
            flops=5 * 10**9, bytes_accessed=8 * 2**20, transcendentals=2**20
        ),
        name="attention_grads",
    )(place, moved, moved, moved, moved, *pieces)


def projection_kernel(place, g_ref, *refs):
    pieces, o_ref = refs[:8], refs[8]
    x_at, z_at, core = place[0], place[1], place[2]
    total = jnp.zeros((ROWS, PAIR), jnp.float32)
    for d in range(4):
        w = weight_rows(pieces[d], pieces[4 + d], z_at, core, slice(0, 3 * SLICE))
        at = pl.multiple_of(lax.rem(x_at + d, 4) * (3 * SLICE), 3 * SLICE)
        total = total + dot(g_ref[:, pl.ds(at, 3 * SLICE)], w, NT)
    o_ref[...] = total.astype(jnp.bfloat16)


def projection_call(place, grads, pieces):
    grid_spec = pltpu.PrefetchScalarGridSpec(
        num_scalar_prefetch=1,
        grid=(8,),
        in_specs=[pl.BlockSpec((ROWS, 3 * D), lambda i, s: (0, 0))]
        + [pl.BlockSpec((4, 1, 16, D), lambda i, s: (0, i, 0, 0))] * 8,
        out_specs=pl.BlockSpec((ROWS, PAIR), lambda i, s: (0, i)),
    )
    return pl.pallas_call(
        projection_kernel,
        grid_spec=grid_spec,
        out_shape=jax.ShapeDtypeStruct((ROWS, D), jnp.bfloat16),
        compiler_params=pltpu.CompilerParams(vmem_limit_bytes=40 * 2**20),
        cost_estimate=pl.CostEstimate(
            flops=2 * 10**9, bytes_accessed=8 * 2**20, transcendentals=0
        ),
        name="input_projection",
    )(place, grads, *pieces)


def spread(block, axes, perms):
    half = block.shape[0] // 2
    after = lax.ppermute(block, axes, perms(-1))
    before = lax.ppermute(block, axes, perms(1))
    far_a = lax.ppermute(before[:half], axes, perms(1))
    far_b = lax.ppermute(after[half:], axes, perms(-1))
    return [block, after, jnp.concatenate([far_a, far_b], axis=0), before]


def gather_weights(input_weights, output_weight):
    x_at = lax.axis_index("x")
    mine = jnp.concatenate(
        [
            lax.dynamic_slice(input_weights, (0, x_at * 3 * SLICE), (16, 3 * SLICE)),
            lax.dynamic_slice(output_weight, (0, x_at * SLICE), (16, SLICE)),
        ],
        axis=1,
    )
    rows = lax.all_to_all(
        jnp.broadcast_to(mine[None], (8, 16, D)), Y_AXES, 0, 0, tiled=True
    )
    plane = jnp.stack(spread(rows, Z_AXES, z_ring), axis=0)
    own = spread(plane, "x", functools.partial(ring, 4))
    return own + [lax.ppermute(piece, "c", ring(2, 1)) for piece in own]


def sum_weight_grad(partial, factor):
    x_at = lax.axis_index("x")
    pair = lax.all_to_all(partial, "c", 0, 0, tiled=True)
    pair = (pair[0].astype(jnp.float32) + pair[1].astype(jnp.float32)).astype(jnp.bfloat16)

    def for_x(shift):
        return lax.dynamic_index_in_dim(pair, lax.rem(x_at + shift, 4), 0, keepdims=False)

    row = for_x(0).astype(jnp.float32)
    for shift in (2, 1, 3):
        row = row + lax.ppermute(for_x(shift), "x", ring(4, shift)).astype(jnp.float32)
    row = row.astype(jnp.bfloat16).reshape(32, 16, SLICE)
    plane = lax.all_to_all(row, ("yh", "yl", "zl"), 0, 0, tiled=True)
    plane = jnp.sum(plane.astype(jnp.float32), axis=0)
    every = lax.all_to_all(
        jnp.broadcast_to(plane[None], (8, 16, SLICE)), ("zh", "x"), 0, 0, tiled=True
    )
    every = (every[:4] + every[4:]) * factor
    return jnp.swapaxes(every, 0, 1).reshape(16, D)


def on_device(query_rows, key_rows, value_rows, upstream, input_weights, output_weight):
    factor = 1.0 / (8 * math.sqrt(16384))
    place = jnp.stack([lax.axis_index("x"), lax.axis_index("zl"), lax.axis_index("c")]).astype(
        jnp.int32
    )
    pieces = gather_weights(input_weights, output_weight)
    sent = jnp.concatenate(
        [a.reshape(CLIP_LEN, PATCH_BLOCK, D) for a in (query_rows, key_rows, value_rows, upstream)],
        axis=2,
    )
    moved = lax.all_to_all(sent, CLIP_AXES, 0, 0, tiled=True).reshape(ROWS, 4 * D)
    grads, partial = attention_call(place, moved, pieces)
    result = projection_call(place, grads, pieces).reshape(CLIP_LEN, PATCH_BLOCK, D)
    input_gradient = lax.all_to_all(result, CLIP_AXES, 0, 0, tiled=True)
    weight_gradient = sum_weight_grad(partial, factor)
    return (input_gradient.reshape(query_rows.shape), weight_gradient)


def solution(mesh):
    axes = ("yh", "yl", "zl", "c", "zh", "x")
    fine = Mesh(mesh.devices.reshape(2, 4, 4, 2, 2, 4), axes)
    seq, dp = ("yh", "yl", "zl", "c"), ("zh", "x")
    rows = P(dp, seq, None, None)
    return jax.shard_map(
        on_device,
        mesh=fine,
        in_specs=(rows, rows, rows, rows, P(seq, None), P(seq, None)),
        out_specs=(rows, P(seq, None)),
        check_vma=False,
    )
```

```python
import math

import jax
import jax.numpy as jnp
from jax import lax
from jax.experimental import pallas as pl
from jax.experimental.pallas import tpu as pltpu
from jax.sharding import Mesh
from jax.sharding import PartitionSpec as P

D = 1024
HEAD_DIM = 64
CLIP_LEN = 32
PATCH_BLOCK = 8
ROWS = CLIP_LEN * PATCH_BLOCK
SLICE = 256
CLIP_AXES = ("yl", "zl", "c")
PLANE_AXES = ("yh", "yl", "zl")
NEG = -1e30
NN = ((1,), (0,))
NT = ((1,), (1,))


def ring(size, shift):
    return [(i, (i + shift) % size) for i in range(size)]


def dot(a, b, contract):
    return lax.dot_general(a, b, (contract, ((), ())), preferred_element_type=jnp.float32)

def weight_rows(own, sibling, core, columns):
    first = core == 0
    parts = []
    for at in range(8):
        mine, other = own[at, :, columns], sibling[at, :, columns]
        parts.append(jnp.where(first, mine, other))
        parts.append(jnp.where(first, other, mine))
    return jnp.concatenate(parts, axis=0)


def head_only(block, head):
    lane = lax.broadcasted_iota(jnp.int32, block.shape, 1)
    keep = (lane >= head * HEAD_DIM) & (lane < (head + 1) * HEAD_DIM)
    return jnp.where(keep, block, jnp.zeros((), block.dtype))


def forward_kernel(place, q_ref, k_ref, v_ref, u_ref, attention_ref, keep_ref, send_ref, bias):
    core = place[1]

    @pl.when(pl.program_id(0) == 0)
    def _():
        row = lax.broadcasted_iota(jnp.int32, (ROWS, ROWS), 0)
        col = lax.broadcasted_iota(jnp.int32, (ROWS, ROWS), 1)
        bias[...] = jnp.where(lax.rem(row - col + ROWS, PATCH_BLOCK) == 0, 0.0, NEG)

    q, k = q_ref[...], k_ref[...]
    v_t = v_ref[...].T
    context_t = []
    for head in range(4):
        scores = dot(q, head_only(k, head), NT) + bias[...]
        top = jnp.max(scores, axis=1, keepdims=True)
        e = jnp.exp2((scores - top) * (math.log2(math.e) / math.sqrt(HEAD_DIM)))
        attention = e * (1.0 / jnp.sum(e, axis=1, keepdims=True))
        attention_ref[head] = attention
        rows = v_t[head * HEAD_DIM : (head + 1) * HEAD_DIM]
        context_t.append(dot(rows, attention.astype(jnp.bfloat16), NT).astype(jnp.bfloat16))
    context_t = jnp.concatenate(context_t, axis=0)
    dw = dot(context_t, u_ref[...], NN).astype(jnp.bfloat16)
    dw = dw.reshape(8, 2, 16, D)
    halves = dw[:, 0].reshape(128, D), dw[:, 1].reshape(128, D)
    keep = jnp.where(core == 0, halves[0], halves[1])
    send = jnp.where(core == 0, halves[1], halves[0])
    for x in range(4):
        keep_ref[x] = keep[:, x * SLICE : (x + 1) * SLICE]
        send_ref[x] = send[:, x * SLICE : (x + 1) * SLICE]


def forward_call(place, moved):
    def column(base):
        return pl.BlockSpec((ROWS, SLICE), lambda i, s: (0, base + i))

    shares = pl.BlockSpec((4, 128, SLICE), lambda i, s: (0, i, 0))
    return pl.pallas_call(
        forward_kernel,
        grid_spec=pltpu.PrefetchScalarGridSpec(
            num_scalar_prefetch=1,
            grid=(4,),
            in_specs=[
                column(0),
                column(4),
                column(8),
                pl.BlockSpec((ROWS, D), lambda i, s: (0, 3)),
            ],
            out_specs=[pl.BlockSpec((4, ROWS, ROWS), lambda i, s: (i, 0, 0)), shares, shares],
            scratch_shapes=[pltpu.VMEM((ROWS, ROWS), jnp.float32)],
        ),
        out_shape=[
            pltpu.HBM((16, ROWS, ROWS), jnp.float32),
            jax.ShapeDtypeStruct((4, 512, SLICE), jnp.bfloat16),
            jax.ShapeDtypeStruct((4, 512, SLICE), jnp.bfloat16),
        ],
        compiler_params=pltpu.CompilerParams(vmem_limit_bytes=20 * 2**20),
        cost_estimate=pl.CostEstimate(
            flops=2 * 10**9, bytes_accessed=8 * 2**20, transcendentals=2**20
        ),
        name="attention_and_weight_grad",
    )(place, moved, moved, moved, moved)


def backward_kernel(place, attention_ref, q_ref, k_ref, v_ref, u_ref, *refs):
    pieces, g_ref = refs[:8], refs[8]
    x_at, core = place[0], place[1]
    cg = jnp.zeros((ROWS, SLICE), jnp.float32)
    for d in range(4):
        w = weight_rows(pieces[d], pieces[4 + d], core, slice(None))
        at = pl.multiple_of(lax.rem(x_at + d, 4) * SLICE, SLICE)
        cg = cg + dot(u_ref[:, pl.ds(at, SLICE)], w, NT)
    cg = cg.astype(jnp.bfloat16)
    v = v_ref[...]
    q_t, k_t, cg_t = q_ref[...].T, k_ref[...].T, cg.T
    for head in range(4):
        rows = slice(head * HEAD_DIM, (head + 1) * HEAD_DIM)
        attention = attention_ref[head]
        attention_b = attention.astype(jnp.bfloat16)
        grad_scores = dot(cg, head_only(v, head), NT)
        total = jnp.sum(attention * grad_scores, axis=1, keepdims=True)
        score_grad = attention * (grad_scores - total) * (1.0 / math.sqrt(HEAD_DIM))
        score_grad = score_grad.astype(jnp.bfloat16)
        g_ref[0, rows] = dot(k_t[rows], score_grad, NT).astype(jnp.bfloat16)
        g_ref[1, rows] = dot(q_t[rows], score_grad, NN).astype(jnp.bfloat16)
        g_ref[2, rows] = dot(cg_t[rows], attention_b, NN).astype(jnp.bfloat16)


def backward_call(place, attention, moved, pieces):
    def column(base):
        return pl.BlockSpec((ROWS, SLICE), lambda i, s: (0, base + i))

    return pl.pallas_call(
        backward_kernel,
        grid_spec=pltpu.PrefetchScalarGridSpec(
            num_scalar_prefetch=1,
            grid=(4,),
            in_specs=[
                pl.BlockSpec((4, ROWS, ROWS), lambda i, s: (i, 0, 0)),
                column(0),
                column(4),
                column(8),
                pl.BlockSpec((ROWS, D), lambda i, s: (0, 3)),
            ]
            + [pl.BlockSpec((8, 16, SLICE), lambda i, s: (i, 0, 3))] * 8,
            out_specs=pl.BlockSpec((3, SLICE, ROWS), lambda i, s: (0, i, 0)),
        ),
        out_shape=pltpu.HBM((3, D, ROWS), jnp.bfloat16),
        compiler_params=pltpu.CompilerParams(vmem_limit_bytes=20 * 2**20),
        cost_estimate=pl.CostEstimate(
            flops=3 * 10**9, bytes_accessed=10 * 2**20, transcendentals=0
        ),
        name="attention_grads",
    )(place, attention, moved, moved, moved, moved, *pieces)


def projection_kernel(place, g_ref, *refs):
    pieces, o_ref = refs[:8], refs[8]
    x_at, core = place[0], place[1]
    width = 3 * SLICE
    total = jnp.zeros((SLICE, ROWS), jnp.float32)
    for d in range(4):
        w = weight_rows(pieces[d], pieces[4 + d], core, slice(0, width))
        at = pl.multiple_of(lax.rem(x_at + d, 4) * width, width)
        total = total + dot(w, g_ref[pl.ds(at, width)], NN)
    o_ref[...] = total.astype(jnp.bfloat16).T


def projection_call(place, grads, pieces):
    return pl.pallas_call(
        projection_kernel,
        grid_spec=pltpu.PrefetchScalarGridSpec(
            num_scalar_prefetch=1,
            grid=(4,),
            in_specs=[pl.BlockSpec((3 * D, ROWS), lambda i, s: (0, 0))]
            + [pl.BlockSpec((8, 16, D), lambda i, s: (i, 0, 0))] * 8,
            out_specs=pl.BlockSpec((ROWS, SLICE), lambda i, s: (0, i)),
        ),
        out_shape=jax.ShapeDtypeStruct((ROWS, D), jnp.bfloat16),
        compiler_params=pltpu.CompilerParams(vmem_limit_bytes=20 * 2**20),
        cost_estimate=pl.CostEstimate(
            flops=2 * 10**9, bytes_accessed=8 * 2**20, transcendentals=0
        ),
        name="input_projection",
    )(place, grads.reshape(3 * D, ROWS), *pieces)


def gather_plane(input_weights, output_weight):
    x_at = lax.axis_index("x")
    mine = jnp.concatenate(
        [
            lax.dynamic_slice(input_weights, (0, x_at * 3 * SLICE), (16, 3 * SLICE)),
            lax.dynamic_slice(output_weight, (0, x_at * SLICE), (16, SLICE)),
        ],
        axis=1,
    )
    return lax.all_to_all(jnp.broadcast_to(mine[None], (32, 16, D)), PLANE_AXES, 0, 0, tiled=True)


def swap_cores(block):
    return lax.ppermute(block, "c", ring(2, 1))


def spread_x(plane):
    half = plane.shape[0] // 2
    after = lax.ppermute(plane, "x", ring(4, -1))
    before = lax.ppermute(plane, "x", ring(4, 1))
    far_a = lax.ppermute(before[:half], "x", ring(4, 1))
    far_b = lax.ppermute(after[half:], "x", ring(4, -1))
    own = [plane, after, jnp.concatenate([far_a, far_b], axis=0), before]
    return own + [swap_cores(piece) for piece in own]


def sum_cores(keep, send):
    return (keep.astype(jnp.float32) + swap_cores(send).astype(jnp.float32)).astype(jnp.bfloat16)


def gather_x(share):
    x_at = lax.axis_index("x")
    result = jnp.zeros((16, D), jnp.float32)
    for shift in range(4):
        columns = share if shift == 0 else lax.ppermute(share, "x", ring(4, -shift))
        at = lax.rem(x_at + shift, 4) * SLICE
        result = lax.dynamic_update_slice(result, columns, (0, at))
    return result


def on_device(query_rows, key_rows, value_rows, upstream, input_weights, output_weight):
    factor = 1.0 / (8 * math.sqrt(16384))
    place = jnp.stack([lax.axis_index(a) for a in ("x", "c")]).astype(jnp.int32)
    plane = gather_plane(input_weights, output_weight)
    sent = jnp.concatenate(
        [a.reshape(CLIP_LEN, PATCH_BLOCK, D) for a in (query_rows, key_rows, value_rows, upstream)],
        axis=2,
    )
    sent, plane = lax.optimization_barrier((sent, plane))
    moved = lax.all_to_all(sent, CLIP_AXES, 0, 0, tiled=True).reshape(ROWS, 4 * D)
    moved, pieces = lax.optimization_barrier((moved, spread_x(plane)))
    attention, keep, send = forward_call(place, moved)
    attention, steps = lax.optimization_barrier((attention, sum_cores(keep, send)))
    steps = lax.all_to_all(steps, "x", 0, 0, tiled=True)
    grads = backward_call(place, attention, moved, pieces)
    grads, steps = lax.optimization_barrier((grads, steps))
    share = jnp.sum(steps.astype(jnp.float32), axis=0).astype(jnp.bfloat16)
    share = lax.all_to_all(share.reshape(32, 16, SLICE), PLANE_AXES, 0, 0, tiled=True)
    result = projection_call(place, grads, pieces).reshape(CLIP_LEN, PATCH_BLOCK, D)
    share = jnp.sum(share.astype(jnp.float32), axis=0) * factor
    share = share + lax.ppermute(share, "zh", ring(2, 1))
    result, share = lax.optimization_barrier((result, share))
    input_gradient = lax.all_to_all(result, CLIP_AXES, 0, 0, tiled=True)
    weight_gradient = gather_x(share)
    return (input_gradient.reshape(query_rows.shape), weight_gradient)


def solution(mesh):
    axes = ("yh", "yl", "zl", "c", "zh", "x")
    fine = Mesh(mesh.devices.reshape(2, 4, 4, 2, 2, 4), axes)
    seq, dp = ("yh", "yl", "zl", "c"), ("zh", "x")
    rows = P(dp, seq, None, None)
    return jax.shard_map(
        on_device,
        mesh=fine,
        in_specs=(rows, rows, rows, rows, P(seq, None), P(seq, None)),
        out_specs=(rows, P(seq, None)),
        check_vma=False,
    )
```

```python
import math

import jax
import jax.numpy as jnp
from jax import lax
from jax.experimental import pallas as pl
from jax.experimental.pallas import tpu as pltpu
from jax.sharding import Mesh
from jax.sharding import PartitionSpec as P

D = 1024
HEAD_DIM = 64
CLIP_LEN = 32
PATCH_BLOCK = 8
ROWS = CLIP_LEN * PATCH_BLOCK
SLICE = 256
CLIP_AXES = ("yl", "zl", "c")
PLANE_AXES = ("yh", "yl", "zl")
NEG = -1e30
NN = ((1,), (0,))
NT = ((1,), (1,))


def ring(size, shift):
    return [(i, (i + shift) % size) for i in range(size)]


def dot(a, b, contract):
    return lax.dot_general(a, b, (contract, ((), ())), preferred_element_type=jnp.float32)

def weight_rows(own, sibling, core, columns):
    first = core == 0
    parts = []
    for at in range(8):
        mine, other = own[at, :, columns], sibling[at, :, columns]
        parts.append(jnp.where(first, mine, other))
        parts.append(jnp.where(first, other, mine))
    return jnp.concatenate(parts, axis=0)


def head_only(block, head):
    lane = lax.broadcasted_iota(jnp.int32, block.shape, 1)
    keep = (lane >= head * HEAD_DIM) & (lane < (head + 1) * HEAD_DIM)
    return jnp.where(keep, block, jnp.zeros((), block.dtype))


def forward_kernel(place, q_ref, k_ref, v_ref, u_ref, attention_ref, keep_ref, send_ref, bias):
    core = place[1]

    @pl.when(pl.program_id(0) == 0)
    def _():
        row = lax.broadcasted_iota(jnp.int32, (ROWS, ROWS), 0)
        col = lax.broadcasted_iota(jnp.int32, (ROWS, ROWS), 1)
        bias[...] = jnp.where(lax.rem(row - col + ROWS, PATCH_BLOCK) == 0, 0.0, NEG)

    q, k = q_ref[...], k_ref[...]
    v_t = v_ref[...].T
    scores = [dot(q, head_only(k, head), NT) for head in range(4)]
    weights = []
    for head in range(4):
        masked = scores[head] + bias[...]
        top = jnp.max(masked, axis=1, keepdims=True)
        e = jnp.exp2((masked - top) * (math.log2(math.e) / math.sqrt(HEAD_DIM)))
        attention = e * (1.0 / jnp.sum(e, axis=1, keepdims=True))
        attention_ref[head] = attention
        weights.append(attention.astype(jnp.bfloat16))
    context_t = []
    for head in range(4):
        rows = v_t[head * HEAD_DIM : (head + 1) * HEAD_DIM]
        context_t.append(dot(rows, weights[head], NT).astype(jnp.bfloat16))
    context_t = jnp.concatenate(context_t, axis=0)
    dw = dot(context_t, u_ref[...], NN).astype(jnp.bfloat16)
    dw = dw.reshape(8, 2, 16, D)
    halves = dw[:, 0].reshape(128, D), dw[:, 1].reshape(128, D)
    keep_ref[...] = jnp.where(core == 0, halves[0], halves[1])
    send_ref[...] = jnp.where(core == 0, halves[1], halves[0])


def forward_call(place, moved):
    def column(base):
        return pl.BlockSpec((ROWS, SLICE), lambda i, s: (0, base + i))

    shares = pl.BlockSpec((128, D), lambda i, s: (i, 0))
    return pl.pallas_call(
        forward_kernel,
        grid_spec=pltpu.PrefetchScalarGridSpec(
            num_scalar_prefetch=1,
            grid=(4,),
            in_specs=[
                column(0),
                column(4),
                column(8),
                pl.BlockSpec((ROWS, D), lambda i, s: (0, 3)),
            ],
            out_specs=[pl.BlockSpec((4, ROWS, ROWS), lambda i, s: (i, 0, 0)), shares, shares],
            scratch_shapes=[pltpu.VMEM((ROWS, ROWS), jnp.float32)],
        ),
        out_shape=[
            pltpu.HBM((16, ROWS, ROWS), jnp.float32),
            jax.ShapeDtypeStruct((512, D), jnp.bfloat16),
            jax.ShapeDtypeStruct((512, D), jnp.bfloat16),
        ],
        compiler_params=pltpu.CompilerParams(vmem_limit_bytes=20 * 2**20),
        cost_estimate=pl.CostEstimate(
            flops=2 * 10**9, bytes_accessed=8 * 2**20, transcendentals=2**20
        ),
        name="attention_and_weight_grad",
    )(place, moved, moved, moved, moved)


def backward_kernel(place, attention_ref, q_ref, k_ref, v_ref, u_ref, *refs):
    pieces, g_ref = refs[:8], refs[8]
    x_at, core = place[0], place[1]
    cg = jnp.zeros((ROWS, SLICE), jnp.float32)
    for d in range(4):
        w = weight_rows(pieces[d], pieces[4 + d], core, slice(None))
        at = pl.multiple_of(lax.rem(x_at + d, 4) * SLICE, SLICE)
        cg = cg + dot(u_ref[:, pl.ds(at, SLICE)], w, NT)
    cg = cg.astype(jnp.bfloat16)
    v = v_ref[...]
    q_t, k_t, cg_t = q_ref[...].T, k_ref[...].T, cg.T
    grad_scores = [dot(cg, head_only(v, head), NT) for head in range(4)]
    score_grads = []
    for head in range(4):
        attention = attention_ref[head]
        total = jnp.sum(attention * grad_scores[head], axis=1, keepdims=True)
        score_grad = attention * (grad_scores[head] - total) * (1.0 / math.sqrt(HEAD_DIM))
        score_grads.append(score_grad.astype(jnp.bfloat16))
    for head in range(4):
        rows = slice(head * HEAD_DIM, (head + 1) * HEAD_DIM)
        attention_b = attention_ref[head].astype(jnp.bfloat16)
        g_ref[0, rows] = dot(k_t[rows], score_grads[head], NT).astype(jnp.bfloat16)
        g_ref[1, rows] = dot(q_t[rows], score_grads[head], NN).astype(jnp.bfloat16)
        g_ref[2, rows] = dot(cg_t[rows], attention_b, NN).astype(jnp.bfloat16)


def backward_call(place, attention, moved, pieces):
    def column(base):
        return pl.BlockSpec((ROWS, SLICE), lambda i, s: (0, base + i))

    return pl.pallas_call(
        backward_kernel,
        grid_spec=pltpu.PrefetchScalarGridSpec(
            num_scalar_prefetch=1,
            grid=(4,),
            in_specs=[
                pl.BlockSpec((4, ROWS, ROWS), lambda i, s: (i, 0, 0)),
                column(0),
                column(4),
                column(8),
                pl.BlockSpec((ROWS, D), lambda i, s: (0, 3)),
            ]
            + [pl.BlockSpec((8, 16, SLICE), lambda i, s: (i, 0, 3))] * 8,
            out_specs=pl.BlockSpec((3, SLICE, ROWS), lambda i, s: (0, i, 0)),
        ),
        out_shape=pltpu.HBM((3, D, ROWS), jnp.bfloat16),
        compiler_params=pltpu.CompilerParams(vmem_limit_bytes=20 * 2**20),
        cost_estimate=pl.CostEstimate(
            flops=3 * 10**9, bytes_accessed=10 * 2**20, transcendentals=0
        ),
        name="attention_grads",
    )(place, attention, moved, moved, moved, moved, *pieces)


def projection_kernel(place, g_ref, *refs):
    pieces, o_ref = refs[:8], refs[8]
    x_at, core = place[0], place[1]
    width = 3 * SLICE
    total = jnp.zeros((SLICE, ROWS), jnp.float32)
    for d in range(4):
        w = weight_rows(pieces[d], pieces[4 + d], core, slice(0, width))
        at = pl.multiple_of(lax.rem(x_at + d, 4) * width, width)
        total = total + dot(w, g_ref[pl.ds(at, width)], NN)
    o_ref[...] = total.astype(jnp.bfloat16).T


def projection_call(place, grads, pieces):
    return pl.pallas_call(
        projection_kernel,
        grid_spec=pltpu.PrefetchScalarGridSpec(
            num_scalar_prefetch=1,
            grid=(4,),
            in_specs=[pl.BlockSpec((3 * D, ROWS), lambda i, s: (0, 0))]
            + [pl.BlockSpec((8, 16, D), lambda i, s: (i, 0, 0))] * 8,
            out_specs=pl.BlockSpec((ROWS, SLICE), lambda i, s: (0, i)),
        ),
        out_shape=jax.ShapeDtypeStruct((ROWS, D), jnp.bfloat16),
        compiler_params=pltpu.CompilerParams(vmem_limit_bytes=20 * 2**20),
        cost_estimate=pl.CostEstimate(
            flops=2 * 10**9, bytes_accessed=8 * 2**20, transcendentals=0
        ),
        name="input_projection",
    )(place, grads.reshape(3 * D, ROWS), *pieces)


def gather_plane(input_weights, output_weight):
    x_at = lax.axis_index("x")
    mine = jnp.concatenate(
        [
            lax.dynamic_slice(input_weights, (0, x_at * 3 * SLICE), (16, 3 * SLICE)),
            lax.dynamic_slice(output_weight, (0, x_at * SLICE), (16, SLICE)),
        ],
        axis=1,
    )
    return lax.all_to_all(jnp.broadcast_to(mine[None], (32, 16, D)), PLANE_AXES, 0, 0, tiled=True)


def swap_cores(block):
    return lax.ppermute(block, "c", ring(2, 1))


def spread_x(plane):
    half = plane.shape[0] // 2
    after = lax.ppermute(plane, "x", ring(4, -1))
    before = lax.ppermute(plane, "x", ring(4, 1))
    far_a = lax.ppermute(before[:half], "x", ring(4, 1))
    far_b = lax.ppermute(after[half:], "x", ring(4, -1))
    own = [plane, after, jnp.concatenate([far_a, far_b], axis=0), before]
    return own + [swap_cores(piece) for piece in own]


def sum_cores(keep, send):
    return (keep.astype(jnp.float32) + swap_cores(send).astype(jnp.float32)).astype(jnp.bfloat16)


def sum_groups(share):
    for bit in (1, 2):
        share = share + lax.ppermute(share, "x", [(i, i ^ bit) for i in range(4)])
    return share + lax.ppermute(share, "zh", ring(2, 1))


def on_device(query_rows, key_rows, value_rows, upstream, input_weights, output_weight):
    factor = 1.0 / (8 * math.sqrt(16384))
    place = jnp.stack([lax.axis_index(a) for a in ("x", "c")]).astype(jnp.int32)
    plane = gather_plane(input_weights, output_weight)
    sent = jnp.concatenate(
        [a.reshape(CLIP_LEN, PATCH_BLOCK, D) for a in (query_rows, key_rows, value_rows, upstream)],
        axis=2,
    )
    sent, plane = lax.optimization_barrier((sent, plane))
    moved = lax.all_to_all(sent, CLIP_AXES, 0, 0, tiled=True).reshape(ROWS, 4 * D)
    moved, pieces = lax.optimization_barrier((moved, spread_x(plane)))
    attention, keep, send = forward_call(place, moved)
    attention, share = lax.optimization_barrier((attention, sum_cores(keep, send)))
    share = lax.all_to_all(share.reshape(32, 16, D), PLANE_AXES, 0, 0, tiled=True)
    grads = backward_call(place, attention, moved, pieces)
    result = projection_call(place, grads, pieces).reshape(CLIP_LEN, PATCH_BLOCK, D)
    result, share = lax.optimization_barrier((result, share))
    input_gradient = lax.all_to_all(result, CLIP_AXES, 0, 0, tiled=True)
    weight_gradient = sum_groups(jnp.sum(share.astype(jnp.float32), axis=0) * factor)
    return (input_gradient.reshape(query_rows.shape), weight_gradient)


def solution(mesh):
    axes = ("yh", "yl", "zl", "c", "zh", "x")
    fine = Mesh(mesh.devices.reshape(2, 4, 4, 2, 2, 4), axes)
    seq, dp = ("yh", "yl", "zl", "c"), ("zh", "x")
    rows = P(dp, seq, None, None)
    return jax.shard_map(
        on_device,
        mesh=fine,
        in_specs=(rows, rows, rows, rows, P(seq, None), P(seq, None)),
        out_specs=(rows, P(seq, None)),
        check_vma=False,
    )
```

```python
import math

import jax
import jax.numpy as jnp
from jax import lax
from jax.experimental import pallas as pl
from jax.experimental.pallas import tpu as pltpu
from jax.sharding import Mesh
from jax.sharding import PartitionSpec as P

D = 1024
HEAD_DIM = 64
CLIP_LEN = 32
PATCH_BLOCK = 8
ROWS = CLIP_LEN * PATCH_BLOCK
SLICE = 256
CLIP_AXES = ("yl", "zl", "c")
PLANE_AXES = ("yh", "yl", "zl")
NEG = -1e30
NN = ((1,), (0,))
NT = ((1,), (1,))


def ring(size, shift):
    return [(i, (i + shift) % size) for i in range(size)]


def dot(a, b, contract):
    return lax.dot_general(a, b, (contract, ((), ())), preferred_element_type=jnp.float32)

def weight_rows(own, sibling, core, columns):
    first = core == 0
    parts = []
    for at in range(8):
        mine, other = own[at, :, columns], sibling[at, :, columns]
        parts.append(jnp.where(first, mine, other))
        parts.append(jnp.where(first, other, mine))
    return jnp.concatenate(parts, axis=0)


def head_only(block, head):
    lane = lax.broadcasted_iota(jnp.int32, block.shape, 1)
    keep = (lane >= head * HEAD_DIM) & (lane < (head + 1) * HEAD_DIM)
    return jnp.where(keep, block, jnp.zeros((), block.dtype))


def forward_kernel(place, q_ref, k_ref, v_ref, u_ref, attention_ref, keep_ref, send_ref, bias):
    core = place[1]

    @pl.when(pl.program_id(0) == 0)
    def _():
        row = lax.broadcasted_iota(jnp.int32, (ROWS, ROWS), 0)
        col = lax.broadcasted_iota(jnp.int32, (ROWS, ROWS), 1)
        bias[...] = jnp.where(lax.rem(row - col + ROWS, PATCH_BLOCK) == 0, 0.0, NEG)

    q, k = q_ref[...], k_ref[...]
    v_t = v_ref[...].T
    scores = [dot(q, head_only(k, head), NT) for head in range(4)]
    weights = []
    for head in range(4):
        masked = scores[head] + bias[...]
        top = jnp.max(masked, axis=1, keepdims=True)
        e = jnp.exp2((masked - top) * (math.log2(math.e) / math.sqrt(HEAD_DIM)))
        attention = e * (1.0 / jnp.sum(e, axis=1, keepdims=True))
        attention_ref[head] = attention
        weights.append(attention.astype(jnp.bfloat16))
    context_t = []
    for head in range(4):
        rows = v_t[head * HEAD_DIM : (head + 1) * HEAD_DIM]
        context_t.append(dot(rows, weights[head], NT).astype(jnp.bfloat16))
    context_t = jnp.concatenate(context_t, axis=0)
    dw = dot(context_t, u_ref[...], NN).astype(jnp.bfloat16)
    dw = dw.reshape(8, 2, 16, D)
    halves = dw[:, 0].reshape(128, D), dw[:, 1].reshape(128, D)
    keep_ref[...] = jnp.where(core == 0, halves[0], halves[1])
    send_ref[...] = jnp.where(core == 0, halves[1], halves[0])


def forward_call(place, moved):
    def column(base):
        return pl.BlockSpec((ROWS, SLICE), lambda i, s: (0, base + i))

    shares = pl.BlockSpec((128, D), lambda i, s: (i, 0))
    return pl.pallas_call(
        forward_kernel,
        grid_spec=pltpu.PrefetchScalarGridSpec(
            num_scalar_prefetch=1,
            grid=(4,),
            in_specs=[
                column(0),
                column(4),
                column(8),
                pl.BlockSpec((ROWS, D), lambda i, s: (0, 3)),
            ],
            out_specs=[pl.BlockSpec((4, ROWS, ROWS), lambda i, s: (i, 0, 0)), shares, shares],
            scratch_shapes=[pltpu.VMEM((ROWS, ROWS), jnp.float32)],
        ),
        out_shape=[
            pltpu.HBM((16, ROWS, ROWS), jnp.float32),
            jax.ShapeDtypeStruct((512, D), jnp.bfloat16),
            jax.ShapeDtypeStruct((512, D), jnp.bfloat16),
        ],
        compiler_params=pltpu.CompilerParams(vmem_limit_bytes=20 * 2**20),
        cost_estimate=pl.CostEstimate(
            flops=2 * 10**9, bytes_accessed=8 * 2**20, transcendentals=2**20
        ),
        name="attention_and_weight_grad",
    )(place, moved, moved, moved, moved)


def backward_kernel(place, attention_ref, q_ref, k_ref, v_ref, u_ref, *refs):
    pieces, g_ref = refs[:8], refs[8]
    x_at, core = place[0], place[1]
    cg = jnp.zeros((ROWS, SLICE), jnp.float32)
    for d in range(4):
        w = weight_rows(pieces[d], pieces[4 + d], core, slice(None))
        at = pl.multiple_of(lax.rem(x_at + d, 4) * SLICE, SLICE)
        cg = cg + dot(u_ref[:, pl.ds(at, SLICE)], w, NT)
    cg = cg.astype(jnp.bfloat16)
    v = v_ref[...]
    q_t, k_t, cg_t = q_ref[...].T, k_ref[...].T, cg.T
    grad_scores = [dot(cg, head_only(v, head), NT) for head in range(4)]
    score_grads = []
    for head in range(4):
        attention = attention_ref[head]
        total = jnp.sum(attention * grad_scores[head], axis=1, keepdims=True)
        score_grad = attention * (grad_scores[head] - total) * (1.0 / math.sqrt(HEAD_DIM))
        score_grads.append(score_grad.astype(jnp.bfloat16))
    for head in range(4):
        rows = slice(head * HEAD_DIM, (head + 1) * HEAD_DIM)
        attention_b = attention_ref[head].astype(jnp.bfloat16)
        g_ref[0, rows] = dot(k_t[rows], score_grads[head], NT).astype(jnp.bfloat16)
        g_ref[1, rows] = dot(q_t[rows], score_grads[head], NN).astype(jnp.bfloat16)
        g_ref[2, rows] = dot(cg_t[rows], attention_b, NN).astype(jnp.bfloat16)


def backward_call(place, attention, moved, pieces):
    def column(base):
        return pl.BlockSpec((ROWS, SLICE), lambda i, s: (0, base + i))

    return pl.pallas_call(
        backward_kernel,
        grid_spec=pltpu.PrefetchScalarGridSpec(
            num_scalar_prefetch=1,
            grid=(4,),
            in_specs=[
                pl.BlockSpec((4, ROWS, ROWS), lambda i, s: (i, 0, 0)),
                column(0),
                column(4),
                column(8),
                pl.BlockSpec((ROWS, D), lambda i, s: (0, 3)),
            ]
            + [pl.BlockSpec((8, 16, SLICE), lambda i, s: (i, 0, 3))] * 8,
            out_specs=pl.BlockSpec((3, SLICE, ROWS), lambda i, s: (0, i, 0)),
        ),
        out_shape=pltpu.HBM((3, D, ROWS), jnp.bfloat16),
        compiler_params=pltpu.CompilerParams(vmem_limit_bytes=20 * 2**20),
        cost_estimate=pl.CostEstimate(
            flops=3 * 10**9, bytes_accessed=10 * 2**20, transcendentals=0
        ),
        name="attention_grads",
    )(place, attention, moved, moved, moved, moved, *pieces)


def projection_kernel(place, g_ref, *refs):
    pieces, o_ref = refs[:8], refs[8]
    x_at, core = place[0], place[1]
    width = 3 * SLICE
    total = jnp.zeros((SLICE, ROWS), jnp.float32)
    for d in range(4):
        w = weight_rows(pieces[d], pieces[4 + d], core, slice(0, width))
        at = pl.multiple_of(lax.rem(x_at + d, 4) * width, width)
        total = total + dot(w, g_ref[pl.ds(at, width)], NN)
    o_ref[...] = total.astype(jnp.bfloat16).T


def projection_call(place, grads, pieces):
    return pl.pallas_call(
        projection_kernel,
        grid_spec=pltpu.PrefetchScalarGridSpec(
            num_scalar_prefetch=1,
            grid=(4,),
            in_specs=[pl.BlockSpec((3 * D, ROWS), lambda i, s: (0, 0))]
            + [pl.BlockSpec((8, 16, D), lambda i, s: (i, 0, 0))] * 8,
            out_specs=pl.BlockSpec((ROWS, SLICE), lambda i, s: (0, i)),
        ),
        out_shape=jax.ShapeDtypeStruct((ROWS, D), jnp.bfloat16),
        compiler_params=pltpu.CompilerParams(vmem_limit_bytes=20 * 2**20),
        cost_estimate=pl.CostEstimate(
            flops=2 * 10**9, bytes_accessed=8 * 2**20, transcendentals=0
        ),
        name="input_projection",
    )(place, grads.reshape(3 * D, ROWS), *pieces)


def own_columns(input_weights, output_weight):
    x_at = lax.axis_index("x")
    mine = jnp.concatenate(
        [
            lax.dynamic_slice(input_weights, (0, x_at * 3 * SLICE), (16, 3 * SLICE)),
            lax.dynamic_slice(output_weight, (0, x_at * SLICE), (16, SLICE)),
        ],
        axis=1,
    )
    return jnp.broadcast_to(mine[None], (32, 16, D))


def swap_cores(block):
    return lax.ppermute(block, "c", ring(2, 1))


def spread_x(plane):
    half = plane.shape[0] // 2
    after = lax.ppermute(plane, "x", ring(4, -1))
    before = lax.ppermute(plane, "x", ring(4, 1))
    far_a = lax.ppermute(before[:half], "x", ring(4, 1))
    far_b = lax.ppermute(after[half:], "x", ring(4, -1))
    return [plane, after, far_a, far_b, before]


def sum_cores(keep, send):
    return (keep.astype(jnp.float32) + swap_cores(send).astype(jnp.float32)).astype(jnp.bfloat16)


def sum_groups(share):
    for bit in (1, 2):
        share = share + lax.ppermute(share, "x", [(i, i ^ bit) for i in range(4)])
    return share + lax.ppermute(share, "zh", ring(2, 1))


def on_device(query_rows, key_rows, value_rows, upstream, input_weights, output_weight):
    factor = 1.0 / (8 * math.sqrt(16384))
    place = jnp.stack([lax.axis_index(a) for a in ("x", "c")]).astype(jnp.int32)
    columns = own_columns(input_weights, output_weight)
    columns, query_rows, key_rows, value_rows, upstream = lax.optimization_barrier(
        (columns, query_rows, key_rows, value_rows, upstream)
    )
    plane = lax.all_to_all(columns, PLANE_AXES, 0, 0, tiled=True)
    core = lax.axis_index("c")

    def both_frames(rows):
        rows = rows.reshape(CLIP_LEN // 2, 2, PATCH_BLOCK, D)
        mine = lax.dynamic_index_in_dim(rows, core, 1, keepdims=False)
        other = swap_cores(lax.dynamic_index_in_dim(rows, 1 - core, 1, keepdims=False))
        return jnp.stack(
            [jnp.where(core == 0, mine, other), jnp.where(core == 0, other, mine)], axis=1
        )

    sent = jnp.concatenate(
        [both_frames(a) for a in (query_rows, key_rows, value_rows, upstream)], axis=3
    )
    sent, plane = lax.optimization_barrier((sent, plane))
    moved = lax.all_to_all(sent, ("yl", "zl"), 0, 0, tiled=True).reshape(ROWS, 4 * D)
    moved, own = lax.optimization_barrier((moved, spread_x(plane)))
    attention, keep, send = forward_call(place, moved)
    attention, share, own = lax.optimization_barrier((attention, sum_cores(keep, send), own))
    share = lax.all_to_all(share.reshape(32, 16, D), PLANE_AXES, 0, 0, tiled=True)
    own = [own[0], own[1], jnp.concatenate(own[2:4], axis=0), own[4]]
    pieces = own + [swap_cores(piece) for piece in own]
    grads = backward_call(place, attention, moved, pieces)
    result = projection_call(place, grads, pieces).reshape(CLIP_LEN, PATCH_BLOCK, D)
    result, share = lax.optimization_barrier((result, share))
    input_gradient = lax.all_to_all(result, CLIP_AXES, 0, 0, tiled=True)
    weight_gradient = sum_groups(jnp.sum(share.astype(jnp.float32), axis=0) * factor)
    return (input_gradient.reshape(query_rows.shape), weight_gradient)


def solution(mesh):
    axes = ("yh", "yl", "zl", "c", "zh", "x")
    fine = Mesh(mesh.devices.reshape(2, 4, 4, 2, 2, 4), axes)
    seq, dp = ("yh", "yl", "zl", "c"), ("zh", "x")
    rows = P(dp, seq, None, None)
    return jax.shard_map(
        on_device,
        mesh=fine,
        in_specs=(rows, rows, rows, rows, P(seq, None), P(seq, None)),
        out_specs=(rows, P(seq, None)),
        check_vma=False,
    )
```

```python
import math

import jax
import jax.numpy as jnp
from jax import lax
from jax.experimental import pallas as pl
from jax.experimental.pallas import tpu as pltpu
from jax.sharding import Mesh
from jax.sharding import PartitionSpec as P

D = 1024
HEAD_DIM = 64
CLIP_LEN = 32
PATCH_BLOCK = 8
ROWS = CLIP_LEN * PATCH_BLOCK
SLICE = 256
CLIP_AXES = ("yl", "zl", "c")
PLANE_AXES = ("yh", "yl", "zl")
NEG = -1e30
NN = ((1,), (0,))
NT = ((1,), (1,))


def ring(size, shift):
    return [(i, (i + shift) % size) for i in range(size)]


def dot(a, b, contract):
    return lax.dot_general(a, b, (contract, ((), ())), preferred_element_type=jnp.float32)

def weight_rows(own, sibling, core, columns):
    first = core == 0
    parts = []
    for at in range(own.shape[0]):
        mine, other = own[at, :, columns], sibling[at, :, columns]
        parts.append(jnp.where(first, mine, other))
        parts.append(jnp.where(first, other, mine))
    return jnp.concatenate(parts, axis=0)


def head_only(block, head):
    lane = lax.broadcasted_iota(jnp.int32, block.shape, 1)
    keep = (lane >= head * HEAD_DIM) & (lane < (head + 1) * HEAD_DIM)
    return jnp.where(keep, block, jnp.zeros((), block.dtype))


def forward_kernel(place, q_ref, k_ref, v_ref, u_ref, attention_ref, keep_ref, send_ref, bias):
    core = place[1]

    @pl.when(pl.program_id(0) == 0)
    def _():
        row = lax.broadcasted_iota(jnp.int32, (ROWS, ROWS), 0)
        col = lax.broadcasted_iota(jnp.int32, (ROWS, ROWS), 1)
        bias[...] = jnp.where(lax.rem(row - col + ROWS, PATCH_BLOCK) == 0, 0.0, NEG)

    v_t = v_ref[...].T
    scores = []
    for head in range(8):
        lanes = slice(head // 4 * SLICE, head // 4 * SLICE + SLICE)
        scores.append(dot(q_ref[:, lanes], head_only(k_ref[:, lanes], head % 4), NT))
    weights = []
    for head in range(8):
        masked = scores[head] + bias[...]
        top = jnp.max(masked, axis=1, keepdims=True)
        e = jnp.exp2((masked - top) * (math.log2(math.e) / math.sqrt(HEAD_DIM)))
        attention = e * (1.0 / jnp.sum(e, axis=1, keepdims=True))
        attention_ref[head] = attention
        weights.append(attention.astype(jnp.bfloat16))
    context_t = []
    for head in range(8):
        rows = v_t[head * HEAD_DIM : (head + 1) * HEAD_DIM]
        context_t.append(dot(rows, weights[head], NT).astype(jnp.bfloat16))
    context_t = jnp.concatenate(context_t, axis=0)
    dw = dot(context_t, u_ref[...], NN).astype(jnp.bfloat16)
    dw = dw.reshape(16, 2, 16, D)
    halves = dw[:, 0].reshape(256, D), dw[:, 1].reshape(256, D)
    keep_ref[...] = jnp.where(core == 0, halves[0], halves[1])
    send_ref[...] = jnp.where(core == 0, halves[1], halves[0])


def forward_call(place, moved):
    def column(base):
        return pl.BlockSpec((ROWS, 512), lambda i, s: (0, base + i))

    shares = pl.BlockSpec((256, D), lambda i, s: (i, 0))
    return pl.pallas_call(
        forward_kernel,
        grid_spec=pltpu.PrefetchScalarGridSpec(
            num_scalar_prefetch=1,
            grid=(2,),
            in_specs=[
                column(0),
                column(2),
                column(4),
                pl.BlockSpec((ROWS, D), lambda i, s: (0, 3)),
            ],
            out_specs=[pl.BlockSpec((8, ROWS, ROWS), lambda i, s: (i, 0, 0)), shares, shares],
            scratch_shapes=[pltpu.VMEM((ROWS, ROWS), jnp.float32)],
        ),
        out_shape=[
            pltpu.HBM((16, ROWS, ROWS), jnp.float32),
            jax.ShapeDtypeStruct((512, D), jnp.bfloat16),
            jax.ShapeDtypeStruct((512, D), jnp.bfloat16),
        ],
        compiler_params=pltpu.CompilerParams(vmem_limit_bytes=16 * 2**20),
        cost_estimate=pl.CostEstimate(
            flops=2 * 10**9, bytes_accessed=8 * 2**20, transcendentals=2**20
        ),
        name="attention_and_weight_grad",
    )(place, moved, moved, moved, moved)


def backward_kernel(place, attention_ref, q_ref, k_ref, v_ref, u_ref, *refs):
    pieces, g_ref = refs[:8], refs[8]
    x_at, core = place[0], place[1]
    cg = jnp.zeros((ROWS, 2 * SLICE), jnp.float32)
    for d in range(4):
        w = weight_rows(pieces[d], pieces[4 + d], core, slice(None))
        at = pl.multiple_of(lax.rem(x_at + d, 4) * SLICE, SLICE)
        cg = cg + dot(u_ref[:, pl.ds(at, SLICE)], w, NT)
    cg = cg.astype(jnp.bfloat16)
    v = v_ref[...]
    q_t, k_t, cg_t = q_ref[...].T, k_ref[...].T, cg.T
    grad_scores = []
    for head in range(8):
        lanes = slice(head // 4 * SLICE, head // 4 * SLICE + SLICE)
        grad_scores.append(dot(cg[:, lanes], head_only(v[:, lanes], head % 4), NT))
    score_grads = []
    for head in range(8):
        attention = attention_ref[head]
        total = jnp.sum(attention * grad_scores[head], axis=1, keepdims=True)
        score_grad = attention * (grad_scores[head] - total) * (1.0 / math.sqrt(HEAD_DIM))
        score_grads.append(score_grad.astype(jnp.bfloat16))
    for head in range(8):
        rows = slice(head * HEAD_DIM, (head + 1) * HEAD_DIM)
        attention_b = attention_ref[head].astype(jnp.bfloat16)
        g_ref[0, rows] = dot(k_t[rows], score_grads[head], NT).astype(jnp.bfloat16)
        g_ref[1, rows] = dot(q_t[rows], score_grads[head], NN).astype(jnp.bfloat16)
        g_ref[2, rows] = dot(cg_t[rows], attention_b, NN).astype(jnp.bfloat16)


def backward_call(place, attention, moved, pieces):
    def column(base):
        return pl.BlockSpec((ROWS, 2 * SLICE), lambda i, s: (0, base + i))

    return pl.pallas_call(
        backward_kernel,
        grid_spec=pltpu.PrefetchScalarGridSpec(
            num_scalar_prefetch=1,
            grid=(2,),
            in_specs=[
                pl.BlockSpec((8, ROWS, ROWS), lambda i, s: (i, 0, 0)),
                column(0),
                column(2),
                column(4),
                pl.BlockSpec((ROWS, D), lambda i, s: (0, 3)),
            ]
            + [pl.BlockSpec((16, 16, SLICE), lambda i, s: (i, 0, 3))] * 8,
            out_specs=pl.BlockSpec((3, 2 * SLICE, ROWS), lambda i, s: (0, i, 0)),
        ),
        out_shape=pltpu.HBM((3, D, ROWS), jnp.bfloat16),
        compiler_params=pltpu.CompilerParams(vmem_limit_bytes=16 * 2**20),
        cost_estimate=pl.CostEstimate(
            flops=3 * 10**9, bytes_accessed=10 * 2**20, transcendentals=0
        ),
        name="attention_grads",
    )(place, attention, moved, moved, moved, moved, *pieces)


def projection_kernel(place, g_ref, *refs):
    pieces, o_ref = refs[:8], refs[8]
    x_at, core = place[0], place[1]
    width = 3 * SLICE
    total = jnp.zeros((SLICE, ROWS), jnp.float32)
    for d in range(4):
        w = weight_rows(pieces[d], pieces[4 + d], core, slice(0, width))
        at = pl.multiple_of(lax.rem(x_at + d, 4) * width, width)
        total = total + dot(w, g_ref[pl.ds(at, width)], NN)
    o_ref[...] = total.astype(jnp.bfloat16).T


def projection_call(place, grads, pieces):
    return pl.pallas_call(
        projection_kernel,
        grid_spec=pltpu.PrefetchScalarGridSpec(
            num_scalar_prefetch=1,
            grid=(4,),
            in_specs=[pl.BlockSpec((3 * D, ROWS), lambda i, s: (0, 0))]
            + [pl.BlockSpec((8, 16, D), lambda i, s: (i, 0, 0))] * 8,
            out_specs=pl.BlockSpec((ROWS, SLICE), lambda i, s: (0, i)),
        ),
        out_shape=jax.ShapeDtypeStruct((ROWS, D), jnp.bfloat16),
        compiler_params=pltpu.CompilerParams(vmem_limit_bytes=20 * 2**20),
        cost_estimate=pl.CostEstimate(
            flops=2 * 10**9, bytes_accessed=8 * 2**20, transcendentals=0
        ),
        name="input_projection",
    )(place, grads.reshape(3 * D, ROWS), *pieces)


def own_columns(input_weights, output_weight):
    x_at = lax.axis_index("x")
    mine = jnp.concatenate(
        [
            lax.dynamic_slice(input_weights, (0, x_at * 3 * SLICE), (16, 3 * SLICE)),
            lax.dynamic_slice(output_weight, (0, x_at * SLICE), (16, SLICE)),
        ],
        axis=1,
    )
    return jnp.broadcast_to(mine[None], (32, 16, D))


def swap_cores(block):
    return lax.ppermute(block, "c", ring(2, 1))


def spread_x(plane):
    half = plane.shape[0] // 2
    after = lax.ppermute(plane, "x", ring(4, -1))
    before = lax.ppermute(plane, "x", ring(4, 1))
    far_a = lax.ppermute(before[:half], "x", ring(4, 1))
    far_b = lax.ppermute(after[half:], "x", ring(4, -1))
    return [plane, after, far_a, far_b, before]


def sum_cores(keep, send):
    return (keep.astype(jnp.float32) + swap_cores(send).astype(jnp.float32)).astype(jnp.bfloat16)


def sum_groups(share):
    for bit in (1, 2):
        share = share + lax.ppermute(share, "x", [(i, i ^ bit) for i in range(4)])
    return share + lax.ppermute(share, "zh", ring(2, 1))


def on_device(query_rows, key_rows, value_rows, upstream, input_weights, output_weight):
    factor = 1.0 / (8 * math.sqrt(16384))
    place = jnp.stack([lax.axis_index(a) for a in ("x", "c")]).astype(jnp.int32)
    columns = own_columns(input_weights, output_weight)
    columns, query_rows, key_rows, value_rows, upstream = lax.optimization_barrier(
        (columns, query_rows, key_rows, value_rows, upstream)
    )
    plane = lax.all_to_all(columns, PLANE_AXES, 0, 0, tiled=True)
    core = lax.axis_index("c")

    def both_frames(rows):
        rows = rows.reshape(CLIP_LEN // 2, 2, PATCH_BLOCK, D)
        mine = lax.dynamic_index_in_dim(rows, core, 1, keepdims=False)
        other = swap_cores(lax.dynamic_index_in_dim(rows, 1 - core, 1, keepdims=False))
        return jnp.stack(
            [jnp.where(core == 0, mine, other), jnp.where(core == 0, other, mine)], axis=1
        )

    sent = jnp.concatenate(
        [both_frames(a) for a in (query_rows, key_rows, value_rows, upstream)], axis=3
    )
    sent, plane = lax.optimization_barrier((sent, plane))
    moved = lax.all_to_all(sent, ("yl", "zl"), 0, 0, tiled=True).reshape(ROWS, 4 * D)
    moved, own = lax.optimization_barrier((moved, spread_x(plane)))
    attention, keep, send = forward_call(place, moved)
    attention, share, own = lax.optimization_barrier((attention, sum_cores(keep, send), own))
    share = lax.all_to_all(share.reshape(32, 16, D), PLANE_AXES, 0, 0, tiled=True)
    own = [own[0], own[1], jnp.concatenate(own[2:4], axis=0), own[4]]
    pieces = own + [swap_cores(piece) for piece in own]
    grads = backward_call(place, attention, moved, pieces)
    result = projection_call(place, grads, pieces).reshape(CLIP_LEN, PATCH_BLOCK, D)
    result, share = lax.optimization_barrier((result, share))
    input_gradient = lax.all_to_all(result, CLIP_AXES, 0, 0, tiled=True)
    weight_gradient = sum_groups(jnp.sum(share.astype(jnp.float32), axis=0) * factor)
    return (input_gradient.reshape(query_rows.shape), weight_gradient)


def solution(mesh):
    axes = ("yh", "yl", "zl", "c", "zh", "x")
    fine = Mesh(mesh.devices.reshape(2, 4, 4, 2, 2, 4), axes)
    seq, dp = ("yh", "yl", "zl", "c"), ("zh", "x")
    rows = P(dp, seq, None, None)
    return jax.shard_map(
        on_device,
        mesh=fine,
        in_specs=(rows, rows, rows, rows, P(seq, None), P(seq, None)),
        out_specs=(rows, P(seq, None)),
        check_vma=False,
    )
```

```python
import math

import jax
import jax.numpy as jnp
from jax import lax
from jax.experimental import pallas as pl
from jax.experimental.pallas import tpu as pltpu
from jax.sharding import Mesh
from jax.sharding import PartitionSpec as P

D = 1024
HEAD_DIM = 64
CLIP_LEN = 32
PATCH_BLOCK = 8
ROWS = CLIP_LEN * PATCH_BLOCK
SLICE = 256
CLIP_AXES = ("yl", "zl", "c")
PLANE_AXES = ("yh", "yl", "zl")
NEG = -1e30
NN = ((1,), (0,))
NT = ((1,), (1,))


def ring(size, shift):
    return [(i, (i + shift) % size) for i in range(size)]


def dot(a, b, contract):
    return lax.dot_general(a, b, (contract, ((), ())), preferred_element_type=jnp.float32)

def weight_rows(own, sibling, core, columns):
    first = core == 0
    parts = []
    for at in range(own.shape[0]):
        mine, other = own[at, :, columns], sibling[at, :, columns]
        parts.append(jnp.where(first, mine, other))
        parts.append(jnp.where(first, other, mine))
    return jnp.concatenate(parts, axis=0)


def head_only(block, head):
    lane = lax.broadcasted_iota(jnp.int32, block.shape, 1)
    keep = (lane >= head * HEAD_DIM) & (lane < (head + 1) * HEAD_DIM)
    return jnp.where(keep, block, jnp.zeros((), block.dtype))


def forward_kernel(place, q_ref, k_ref, v_ref, u_ref, attention_ref, keep_ref, send_ref, bias):
    core = place[1]

    @pl.when(pl.program_id(0) == 0)
    def _():
        row = lax.broadcasted_iota(jnp.int32, (ROWS, ROWS), 0)
        col = lax.broadcasted_iota(jnp.int32, (ROWS, ROWS), 1)
        bias[...] = jnp.where(lax.rem(row - col + ROWS, PATCH_BLOCK) == 0, 0.0, NEG)

    v_t = v_ref[...].T
    scores = []
    for head in range(8):
        lanes = slice(head // 4 * SLICE, head // 4 * SLICE + SLICE)
        scores.append(dot(q_ref[:, lanes], head_only(k_ref[:, lanes], head % 4), NT))
    weights = []
    for head in range(8):
        masked = scores[head] + bias[...]
        top = jnp.max(masked, axis=1, keepdims=True)
        e = jnp.exp2((masked - top) * (math.log2(math.e) / math.sqrt(HEAD_DIM)))
        attention = e * (1.0 / jnp.sum(e, axis=1, keepdims=True))
        attention_ref[head] = attention
        weights.append(attention.astype(jnp.bfloat16))
    context_t = []
    for head in range(8):
        rows = v_t[head * HEAD_DIM : (head + 1) * HEAD_DIM]
        context_t.append(dot(rows, weights[head], NT).astype(jnp.bfloat16))
    context_t = jnp.concatenate(context_t, axis=0)
    dw = dot(context_t, u_ref[...], NN).astype(jnp.bfloat16)
    dw = dw.reshape(16, 2, 16, D)
    halves = dw[:, 0].reshape(256, D), dw[:, 1].reshape(256, D)
    keep_ref[...] = jnp.where(core == 0, halves[0], halves[1])
    send_ref[...] = jnp.where(core == 0, halves[1], halves[0])


def forward_call(place, moved):
    def column(base):
        return pl.BlockSpec((ROWS, 512), lambda i, s: (0, base + i))

    shares = pl.BlockSpec((256, D), lambda i, s: (i, 0))
    return pl.pallas_call(
        forward_kernel,
        grid_spec=pltpu.PrefetchScalarGridSpec(
            num_scalar_prefetch=1,
            grid=(2,),
            in_specs=[
                column(0),
                column(2),
                column(4),
                pl.BlockSpec((ROWS, D), lambda i, s: (0, 3)),
            ],
            out_specs=[pl.BlockSpec((8, ROWS, ROWS), lambda i, s: (i, 0, 0)), shares, shares],
            scratch_shapes=[pltpu.VMEM((ROWS, ROWS), jnp.float32)],
        ),
        out_shape=[
            pltpu.HBM((16, ROWS, ROWS), jnp.float32),
            jax.ShapeDtypeStruct((512, D), jnp.bfloat16),
            jax.ShapeDtypeStruct((512, D), jnp.bfloat16),
        ],
        compiler_params=pltpu.CompilerParams(vmem_limit_bytes=16 * 2**20),
        cost_estimate=pl.CostEstimate(
            flops=2 * 10**9, bytes_accessed=8 * 2**20, transcendentals=2**20
        ),
        name="attention_and_weight_grad",
    )(place, moved, moved, moved, moved)


def backward_kernel(place, attention_ref, q_ref, k_ref, v_ref, u_ref, *refs):
    pieces, g_ref = refs[:8], refs[8]
    x_at, core = place[0], place[1]
    cg = jnp.zeros((ROWS, 2 * SLICE), jnp.float32)
    for d in range(4):
        w = weight_rows(pieces[d], pieces[4 + d], core, slice(None))
        at = pl.multiple_of(lax.rem(x_at + d, 4) * SLICE, SLICE)
        cg = cg + dot(u_ref[:, pl.ds(at, SLICE)], w, NT)
    cg = cg.astype(jnp.bfloat16)
    v = v_ref[...]
    q_t, k_t, cg_t = q_ref[...].T, k_ref[...].T, cg.T
    grad_scores = []
    for head in range(8):
        lanes = slice(head // 4 * SLICE, head // 4 * SLICE + SLICE)
        grad_scores.append(dot(cg[:, lanes], head_only(v[:, lanes], head % 4), NT))
    score_grads = []
    for head in range(8):
        attention = attention_ref[head]
        total = jnp.sum(attention * grad_scores[head], axis=1, keepdims=True)
        score_grad = attention * (grad_scores[head] - total) * (1.0 / math.sqrt(HEAD_DIM))
        score_grads.append(score_grad.astype(jnp.bfloat16))
    for head in range(8):
        rows = slice(head * HEAD_DIM, (head + 1) * HEAD_DIM)
        attention_b = attention_ref[head].astype(jnp.bfloat16)
        g_ref[0, rows] = dot(k_t[rows], score_grads[head], NT).astype(jnp.bfloat16)
        g_ref[1, rows] = dot(q_t[rows], score_grads[head], NN).astype(jnp.bfloat16)
        g_ref[2, rows] = dot(cg_t[rows], attention_b, NN).astype(jnp.bfloat16)


def backward_call(place, attention, moved, pieces):
    def column(base):
        return pl.BlockSpec((ROWS, 2 * SLICE), lambda i, s: (0, base + i))

    return pl.pallas_call(
        backward_kernel,
        grid_spec=pltpu.PrefetchScalarGridSpec(
            num_scalar_prefetch=1,
            grid=(2,),
            in_specs=[
                pl.BlockSpec((8, ROWS, ROWS), lambda i, s: (i, 0, 0)),
                column(0),
                column(2),
                column(4),
                pl.BlockSpec((ROWS, D), lambda i, s: (0, 3)),
            ]
            + [pl.BlockSpec((16, 16, SLICE), lambda i, s: (i, 0, 3))] * 8,
            out_specs=pl.BlockSpec((3, 2 * SLICE, ROWS), lambda i, s: (0, i, 0)),
        ),
        out_shape=jax.ShapeDtypeStruct((3, D, ROWS), jnp.bfloat16),
        compiler_params=pltpu.CompilerParams(vmem_limit_bytes=16 * 2**20),
        cost_estimate=pl.CostEstimate(
            flops=3 * 10**9, bytes_accessed=10 * 2**20, transcendentals=0
        ),
        name="attention_grads",
    )(place, attention, moved, moved, moved, moved, *pieces)


def projection_kernel(place, g_ref, *refs):
    pieces, o_ref = refs[:8], refs[8]
    x_at, core = place[0], place[1]
    width = 3 * SLICE
    total = jnp.zeros((SLICE, ROWS), jnp.float32)
    for d in range(4):
        w = weight_rows(pieces[d], pieces[4 + d], core, slice(0, width))
        at = pl.multiple_of(lax.rem(x_at + d, 4) * width, width)
        total = total + dot(w, g_ref[pl.ds(at, width)], NN)
    o_ref[...] = total.astype(jnp.bfloat16).T


def projection_call(place, grads, pieces):
    return pl.pallas_call(
        projection_kernel,
        grid_spec=pltpu.PrefetchScalarGridSpec(
            num_scalar_prefetch=1,
            grid=(4,),
            in_specs=[pl.BlockSpec((3 * D, ROWS), lambda i, s: (0, 0))]
            + [pl.BlockSpec((8, 16, D), lambda i, s: (i, 0, 0))] * 8,
            out_specs=pl.BlockSpec((ROWS, SLICE), lambda i, s: (0, i)),
        ),
        out_shape=jax.ShapeDtypeStruct((ROWS, D), jnp.bfloat16),
        compiler_params=pltpu.CompilerParams(vmem_limit_bytes=20 * 2**20),
        cost_estimate=pl.CostEstimate(
            flops=2 * 10**9, bytes_accessed=8 * 2**20, transcendentals=0
        ),
        name="input_projection",
    )(place, grads.reshape(3 * D, ROWS), *pieces)


def own_columns(input_weights, output_weight):
    x_at = lax.axis_index("x")
    mine = jnp.concatenate(
        [
            lax.dynamic_slice(input_weights, (0, x_at * 3 * SLICE), (16, 3 * SLICE)),
            lax.dynamic_slice(output_weight, (0, x_at * SLICE), (16, SLICE)),
        ],
        axis=1,
    )
    return jnp.broadcast_to(mine[None], (32, 16, D))


def swap_cores(block):
    return lax.ppermute(block, "c", ring(2, 1))


def spread_x(plane):
    half = plane.shape[0] // 2
    after = lax.ppermute(plane, "x", ring(4, -1))
    before = lax.ppermute(plane, "x", ring(4, 1))
    far_a = lax.ppermute(before[:half], "x", ring(4, 1))
    far_b = lax.ppermute(after[half:], "x", ring(4, -1))
    return [plane, after, far_a, far_b, before]


def sum_cores(keep, send):
    return (keep.astype(jnp.float32) + swap_cores(send).astype(jnp.float32)).astype(jnp.bfloat16)


def sum_groups(share):
    for bit in (1, 2):
        share = share + lax.ppermute(share, "x", [(i, i ^ bit) for i in range(4)])
    return share + lax.ppermute(share, "zh", ring(2, 1))


def on_device(query_rows, key_rows, value_rows, upstream, input_weights, output_weight):
    factor = 1.0 / (8 * math.sqrt(16384))
    place = jnp.stack([lax.axis_index(a) for a in ("x", "c")]).astype(jnp.int32)
    columns = own_columns(input_weights, output_weight)
    columns, query_rows, key_rows, value_rows, upstream = lax.optimization_barrier(
        (columns, query_rows, key_rows, value_rows, upstream)
    )
    plane = lax.all_to_all(columns, PLANE_AXES, 0, 0, tiled=True)
    sent = jnp.concatenate(
        [a.reshape(CLIP_LEN, PATCH_BLOCK, D) for a in (query_rows, key_rows, value_rows, upstream)],
        axis=2,
    )
    sent, plane = lax.optimization_barrier((sent, plane))
    moved = lax.all_to_all(sent, CLIP_AXES, 0, 0, tiled=True).reshape(ROWS, 4 * D)
    moved, own = lax.optimization_barrier((moved, spread_x(plane)))
    attention, keep, send = forward_call(place, moved)
    attention, share, own = lax.optimization_barrier((attention, sum_cores(keep, send), own))
    share = lax.all_to_all(share.reshape(32, 16, D), PLANE_AXES, 0, 0, tiled=True)
    own = [own[0], own[1], jnp.concatenate(own[2:4], axis=0), own[4]]
    pieces = own + [swap_cores(piece) for piece in own]
    grads = backward_call(place, attention, moved, pieces)
    result = projection_call(place, grads, pieces).reshape(CLIP_LEN, PATCH_BLOCK, D)
    result, share = lax.optimization_barrier((result, share))
    input_gradient = lax.all_to_all(result, CLIP_AXES, 0, 0, tiled=True)
    weight_gradient = sum_groups(jnp.sum(share.astype(jnp.float32), axis=0) * factor)
    return (input_gradient.reshape(query_rows.shape), weight_gradient)


def solution(mesh):
    axes = ("yh", "yl", "zl", "c", "zh", "x")
    fine = Mesh(mesh.devices.reshape(2, 4, 4, 2, 2, 4), axes)
    seq, dp = ("yh", "yl", "zl", "c"), ("zh", "x")
    rows = P(dp, seq, None, None)
    return jax.shard_map(
        on_device,
        mesh=fine,
        in_specs=(rows, rows, rows, rows, P(seq, None), P(seq, None)),
        out_specs=(rows, P(seq, None)),
        check_vma=False,
    )
```

```python
import math

import jax
import jax.numpy as jnp
from jax import lax
from jax.experimental import pallas as pl
from jax.experimental.pallas import tpu as pltpu
from jax.sharding import Mesh
from jax.sharding import PartitionSpec as P

D = 1024
HEAD_DIM = 64
CLIP_LEN = 32
PATCH_BLOCK = 8
ROWS = CLIP_LEN * PATCH_BLOCK
SLICE = 256
CLIP_AXES = ("yl", "zl", "c")
PLANE_AXES = ("yh", "yl", "zl")
NEG = -1e30
NN = ((1,), (0,))
NT = ((1,), (1,))


def ring(size, shift):
    return [(i, (i + shift) % size) for i in range(size)]


def dot(a, b, contract):
    return lax.dot_general(a, b, (contract, ((), ())), preferred_element_type=jnp.float32)

def weight_rows(own, sibling, core, columns):
    first = core == 0
    parts = []
    for at in range(own.shape[0]):
        mine, other = own[at, :, columns], sibling[at, :, columns]
        parts.append(jnp.where(first, mine, other))
        parts.append(jnp.where(first, other, mine))
    return jnp.concatenate(parts, axis=0)


def head_only(block, head):
    lane = lax.broadcasted_iota(jnp.int32, block.shape, 1)
    keep = (lane >= head * HEAD_DIM) & (lane < (head + 1) * HEAD_DIM)
    return jnp.where(keep, block, jnp.zeros((), block.dtype))


def forward_kernel(place, q_ref, k_ref, v_ref, u_ref, attention_ref, keep_ref, send_ref, bias):
    core = place[1]

    @pl.when(pl.program_id(0) == 0)
    def _():
        row = lax.broadcasted_iota(jnp.int32, (ROWS, ROWS), 0)
        col = lax.broadcasted_iota(jnp.int32, (ROWS, ROWS), 1)
        bias[...] = jnp.where(lax.rem(row - col + ROWS, PATCH_BLOCK) == 0, 0.0, NEG)

    v_t = v_ref[...].T
    scores = []
    for head in range(8):
        lanes = slice(head // 4 * SLICE, head // 4 * SLICE + SLICE)
        scores.append(dot(q_ref[:, lanes], head_only(k_ref[:, lanes], head % 4), NT))
    weights = []
    for head in range(8):
        masked = scores[head] + bias[...]
        top = jnp.max(masked, axis=1, keepdims=True)
        e = jnp.exp2((masked - top) * (math.log2(math.e) / math.sqrt(HEAD_DIM)))
        attention = e * (1.0 / jnp.sum(e, axis=1, keepdims=True))
        attention_ref[head] = attention
        weights.append(attention.astype(jnp.bfloat16))
    context_t = []
    for head in range(8):
        rows = v_t[head * HEAD_DIM : (head + 1) * HEAD_DIM]
        context_t.append(dot(rows, weights[head], NT).astype(jnp.bfloat16))
    context_t = jnp.concatenate(context_t, axis=0)
    dw = dot(context_t, u_ref[...], NN).astype(jnp.bfloat16)
    dw = dw.reshape(16, 2, 16, D)
    halves = dw[:, 0].reshape(256, D), dw[:, 1].reshape(256, D)
    keep_ref[...] = jnp.where(core == 0, halves[0], halves[1])
    send_ref[...] = jnp.where(core == 0, halves[1], halves[0])


def forward_call(place, moved):
    def column(base):
        return pl.BlockSpec((ROWS, 512), lambda i, s: (0, base + i))

    shares = pl.BlockSpec((256, D), lambda i, s: (i, 0))
    return pl.pallas_call(
        forward_kernel,
        grid_spec=pltpu.PrefetchScalarGridSpec(
            num_scalar_prefetch=1,
            grid=(2,),
            in_specs=[
                column(0),
                column(2),
                column(4),
                pl.BlockSpec((ROWS, D), lambda i, s: (0, 3)),
            ],
            out_specs=[pl.BlockSpec((8, ROWS, ROWS), lambda i, s: (i, 0, 0)), shares, shares],
            scratch_shapes=[pltpu.VMEM((ROWS, ROWS), jnp.float32)],
        ),
        out_shape=[
            pltpu.HBM((16, ROWS, ROWS), jnp.float32),
            jax.ShapeDtypeStruct((512, D), jnp.bfloat16),
            jax.ShapeDtypeStruct((512, D), jnp.bfloat16),
        ],
        compiler_params=pltpu.CompilerParams(vmem_limit_bytes=16 * 2**20),
        cost_estimate=pl.CostEstimate(
            flops=2 * 10**9, bytes_accessed=8 * 2**20, transcendentals=2**20
        ),
        name="attention_and_weight_grad",
    )(place, moved, moved, moved, moved)


def backward_kernel(place, attention_ref, q_ref, k_ref, v_ref, u_ref, *refs):
    pieces, g_ref = refs[:8], refs[8]
    x_at, core = place[0], place[1]
    cg = jnp.zeros((ROWS, 2 * SLICE), jnp.float32)
    for d in range(4):
        w = weight_rows(pieces[d], pieces[4 + d], core, slice(None))
        at = pl.multiple_of(lax.rem(x_at + d, 4) * SLICE, SLICE)
        cg = cg + dot(u_ref[:, pl.ds(at, SLICE)], w, NT)
    cg = cg.astype(jnp.bfloat16)
    v = v_ref[...]
    q_t, k_t, cg_t = q_ref[...].T, k_ref[...].T, cg.T
    grad_scores = []
    for head in range(8):
        lanes = slice(head // 4 * SLICE, head // 4 * SLICE + SLICE)
        grad_scores.append(dot(cg[:, lanes], head_only(v[:, lanes], head % 4), NT))
    score_grads = []
    for head in range(8):
        attention = attention_ref[head]
        total = jnp.sum(attention * grad_scores[head], axis=1, keepdims=True)
        score_grad = attention * (grad_scores[head] - total) * (1.0 / math.sqrt(HEAD_DIM))
        score_grads.append(score_grad.astype(jnp.bfloat16))
    for head in range(8):
        rows = slice(head * HEAD_DIM, (head + 1) * HEAD_DIM)
        attention_b = attention_ref[head].astype(jnp.bfloat16)
        g_ref[0, rows] = dot(k_t[rows], score_grads[head], NT).astype(jnp.bfloat16)
        g_ref[1, rows] = dot(q_t[rows], score_grads[head], NN).astype(jnp.bfloat16)
        g_ref[2, rows] = dot(cg_t[rows], attention_b, NN).astype(jnp.bfloat16)


def backward_call(place, attention, moved, pieces):
    def column(base):
        return pl.BlockSpec((ROWS, 2 * SLICE), lambda i, s: (0, base + i))

    return pl.pallas_call(
        backward_kernel,
        grid_spec=pltpu.PrefetchScalarGridSpec(
            num_scalar_prefetch=1,
            grid=(2,),
            in_specs=[
                pl.BlockSpec((8, ROWS, ROWS), lambda i, s: (i, 0, 0)),
                column(0),
                column(2),
                column(4),
                pl.BlockSpec((ROWS, D), lambda i, s: (0, 3)),
            ]
            + [pl.BlockSpec((16, 16, SLICE), lambda i, s: (i, 0, 3))] * 8,
            out_specs=pl.BlockSpec((3, 2 * SLICE, ROWS), lambda i, s: (0, i, 0)),
        ),
        out_shape=jax.ShapeDtypeStruct((3, D, ROWS), jnp.bfloat16),
        compiler_params=pltpu.CompilerParams(vmem_limit_bytes=16 * 2**20),
        cost_estimate=pl.CostEstimate(
            flops=3 * 10**9, bytes_accessed=10 * 2**20, transcendentals=0
        ),
        name="attention_grads",
    )(place, attention, moved, moved, moved, moved, *pieces)


def projection_kernel(place, g_ref, *refs):
    pieces, o_ref = refs[:8], refs[8]
    x_at, core = place[0], place[1]
    width = 3 * SLICE
    total = jnp.zeros((SLICE, ROWS), jnp.float32)
    for d in range(4):
        w = weight_rows(pieces[d], pieces[4 + d], core, slice(0, width))
        at = pl.multiple_of(lax.rem(x_at + d, 4) * width, width)
        total = total + dot(w, g_ref[pl.ds(at, width)], NN)
    o_ref[...] = total.astype(jnp.bfloat16).T


def projection_call(place, grads, pieces):
    return pl.pallas_call(
        projection_kernel,
        grid_spec=pltpu.PrefetchScalarGridSpec(
            num_scalar_prefetch=1,
            grid=(4,),
            in_specs=[pl.BlockSpec((3 * D, ROWS), lambda i, s: (0, 0))]
            + [pl.BlockSpec((8, 16, D), lambda i, s: (i, 0, 0))] * 8,
            out_specs=pl.BlockSpec((ROWS, SLICE), lambda i, s: (0, i)),
        ),
        out_shape=jax.ShapeDtypeStruct((ROWS, D), jnp.bfloat16),
        compiler_params=pltpu.CompilerParams(vmem_limit_bytes=20 * 2**20),
        cost_estimate=pl.CostEstimate(
            flops=2 * 10**9, bytes_accessed=8 * 2**20, transcendentals=0
        ),
        name="input_projection",
    )(place, grads.reshape(3 * D, ROWS), *pieces)


def own_columns(input_weights, output_weight):
    x_at = lax.axis_index("x")
    mine = jnp.concatenate(
        [
            lax.dynamic_slice(input_weights, (0, x_at * 3 * SLICE), (16, 3 * SLICE)),
            lax.dynamic_slice(output_weight, (0, x_at * SLICE), (16, SLICE)),
        ],
        axis=1,
    )
    return jnp.broadcast_to(mine[None], (32, 16, D))


def swap_cores(block):
    return lax.ppermute(block, "c", ring(2, 1))


def spread_x(plane):
    half = plane.shape[0] // 2
    after = lax.ppermute(plane, "x", ring(4, -1))
    before = lax.ppermute(plane, "x", ring(4, 1))
    far_a = lax.ppermute(before[:half], "x", ring(4, 1))
    far_b = lax.ppermute(after[half:], "x", ring(4, -1))
    return [plane, after, far_a, far_b, before]


def sum_cores(keep, send):
    return (keep.astype(jnp.float32) + swap_cores(send).astype(jnp.float32)).astype(jnp.bfloat16)


def write_kernel(i_ref, o_ref):
    o_ref[...] = i_ref[...]


def write_out(rows):
    block = pl.BlockSpec((64, D), lambda i: (i, 0))
    return pl.pallas_call(
        write_kernel,
        grid=(4,),
        in_specs=[block],
        out_specs=block,
        out_shape=jax.ShapeDtypeStruct(rows.shape, rows.dtype),
        compiler_params=pltpu.CompilerParams(vmem_limit_bytes=8 * 2**20),
        name="write_out",
    )(rows)


def sum_x(share):
    for bit in (1, 2):
        share = share + lax.ppermute(share, "x", [(i, i ^ bit) for i in range(4)])
    return share


def on_device(query_rows, key_rows, value_rows, upstream, input_weights, output_weight):
    factor = 1.0 / (8 * math.sqrt(16384))
    place = jnp.stack([lax.axis_index(a) for a in ("x", "c")]).astype(jnp.int32)
    columns = own_columns(input_weights, output_weight)
    columns, query_rows, key_rows, value_rows, upstream = lax.optimization_barrier(
        (columns, query_rows, key_rows, value_rows, upstream)
    )
    plane = lax.all_to_all(columns, PLANE_AXES, 0, 0, tiled=True)
    sent = jnp.concatenate(
        [a.reshape(CLIP_LEN, PATCH_BLOCK, D) for a in (query_rows, key_rows, value_rows, upstream)],
        axis=2,
    )
    sent, plane = lax.optimization_barrier((sent, plane))
    moved = lax.all_to_all(sent, CLIP_AXES, 0, 0, tiled=True).reshape(ROWS, 4 * D)
    moved, own = lax.optimization_barrier((moved, spread_x(plane)))
    attention, keep, send = forward_call(place, moved)
    attention, share, own = lax.optimization_barrier((attention, sum_cores(keep, send), own))
    share = lax.all_to_all(share.reshape(32, 16, D), PLANE_AXES, 0, 0, tiled=True)
    own = [own[0], own[1], jnp.concatenate(own[2:4], axis=0), own[4]]
    pieces = own + [swap_cores(piece) for piece in own]
    grads = backward_call(place, attention, moved, pieces)
    result = projection_call(place, grads, pieces).reshape(CLIP_LEN, PATCH_BLOCK, D)
    result, share = lax.optimization_barrier((result, share))
    input_gradient = lax.all_to_all(result, CLIP_AXES, 0, 0, tiled=True)
    share = sum_x(jnp.sum(share.astype(jnp.float32), axis=0) * factor)
    other = lax.ppermute(share, "zh", ring(2, 1))
    input_gradient = write_out(input_gradient.reshape(ROWS, D))
    input_gradient, other = lax.optimization_barrier((input_gradient, other))
    weight_gradient = share + other
    return (input_gradient.reshape(query_rows.shape), weight_gradient)


def solution(mesh):
    axes = ("yh", "yl", "zl", "c", "zh", "x")
    fine = Mesh(mesh.devices.reshape(2, 4, 4, 2, 2, 4), axes)
    seq, dp = ("yh", "yl", "zl", "c"), ("zh", "x")
    rows = P(dp, seq, None, None)
    return jax.shard_map(
        on_device,
        mesh=fine,
        in_specs=(rows, rows, rows, rows, P(seq, None), P(seq, None)),
        out_specs=(rows, P(seq, None)),
        check_vma=False,
    )
```

```python
import functools
import math

import jax
import jax.numpy as jnp
from jax import lax
from jax.experimental import pallas as pl
from jax.experimental.pallas import tpu as pltpu
from jax.sharding import Mesh
from jax.sharding import PartitionSpec as P

D = 1024
HEAD_DIM = 64
CLIP_LEN = 32
PATCH_BLOCK = 8
ROWS = CLIP_LEN * PATCH_BLOCK
SLICE = 256
CLIP_AXES = ("yl", "zl", "c")
PLANE_AXES = ("yh", "yl", "zl")
NEG = -1e30
NN = ((1,), (0,))
NT = ((1,), (1,))


def ring(size, shift):
    return [(i, (i + shift) % size) for i in range(size)]


def dot(a, b, contract):
    return lax.dot_general(a, b, (contract, ((), ())), preferred_element_type=jnp.float32)

def weight_rows(own, sibling, core, columns):
    first = core == 0
    parts = []
    for at in range(own.shape[0]):
        mine, other = own[at, :, columns], sibling[at, :, columns]
        parts.append(jnp.where(first, mine, other))
        parts.append(jnp.where(first, other, mine))
    return jnp.concatenate(parts, axis=0)


def head_only(block, head):
    lane = lax.broadcasted_iota(jnp.int32, block.shape, 1)
    keep = (lane >= head * HEAD_DIM) & (lane < (head + 1) * HEAD_DIM)
    return jnp.where(keep, block, jnp.zeros((), block.dtype))


def forward_kernel(place, q_ref, k_ref, v_ref, u_ref, attention_ref, keep_ref, send_ref, bias):
    core = place[1]

    @pl.when(pl.program_id(0) == 0)
    def _():
        row = lax.broadcasted_iota(jnp.int32, (ROWS, ROWS), 0)
        col = lax.broadcasted_iota(jnp.int32, (ROWS, ROWS), 1)
        bias[...] = jnp.where(lax.rem(row - col + ROWS, PATCH_BLOCK) == 0, 0.0, NEG)

    v_t = v_ref[...].T
    scores = []
    for head in range(8):
        lanes = slice(head // 4 * SLICE, head // 4 * SLICE + SLICE)
        scores.append(dot(q_ref[:, lanes], head_only(k_ref[:, lanes], head % 4), NT))
    weights = []
    for head in range(8):
        masked = scores[head] + bias[...]
        top = jnp.max(masked, axis=1, keepdims=True)
        e = jnp.exp2((masked - top) * (math.log2(math.e) / math.sqrt(HEAD_DIM)))
        attention = e * (1.0 / jnp.sum(e, axis=1, keepdims=True))
        attention_ref[head] = attention
        weights.append(attention.astype(jnp.bfloat16))
    context_t = []
    for head in range(8):
        rows = v_t[head * HEAD_DIM : (head + 1) * HEAD_DIM]
        context_t.append(dot(rows, weights[head], NT).astype(jnp.bfloat16))
    context_t = jnp.concatenate(context_t, axis=0)
    dw = dot(context_t, u_ref[...], NN).astype(jnp.bfloat16)
    dw = dw.reshape(16, 2, 16, D)
    halves = dw[:, 0].reshape(256, D), dw[:, 1].reshape(256, D)
    keep_ref[...] = jnp.where(core == 0, halves[0], halves[1])
    send_ref[...] = jnp.where(core == 0, halves[1], halves[0])


def forward_call(place, moved):
    def column(base):
        return pl.BlockSpec((ROWS, 512), lambda i, s: (0, base + i))

    shares = pl.BlockSpec((256, D), lambda i, s: (i, 0))
    return pl.pallas_call(
        forward_kernel,
        grid_spec=pltpu.PrefetchScalarGridSpec(
            num_scalar_prefetch=1,
            grid=(2,),
            in_specs=[
                column(0),
                column(2),
                column(4),
                pl.BlockSpec((ROWS, D), lambda i, s: (0, 3)),
            ],
            out_specs=[pl.BlockSpec((8, ROWS, ROWS), lambda i, s: (i, 0, 0)), shares, shares],
            scratch_shapes=[pltpu.VMEM((ROWS, ROWS), jnp.float32)],
        ),
        out_shape=[
            pltpu.HBM((16, ROWS, ROWS), jnp.float32),
            jax.ShapeDtypeStruct((512, D), jnp.bfloat16),
            jax.ShapeDtypeStruct((512, D), jnp.bfloat16),
        ],
        compiler_params=pltpu.CompilerParams(vmem_limit_bytes=16 * 2**20),
        cost_estimate=pl.CostEstimate(
            flops=2 * 10**9, bytes_accessed=8 * 2**20, transcendentals=2**20
        ),
        name="attention_and_weight_grad",
    )(place, moved, moved, moved, moved)


def backward_kernel(place, attention_ref, q_ref, k_ref, v_ref, u_ref, *refs):
    pieces, g_ref = refs[:8], refs[8]
    x_at, core = place[0], place[1]
    cg = jnp.zeros((ROWS, 2 * SLICE), jnp.float32)
    for d in range(4):
        w = weight_rows(pieces[d], pieces[4 + d], core, slice(None))
        at = pl.multiple_of(lax.rem(x_at + d, 4) * SLICE, SLICE)
        cg = cg + dot(u_ref[:, pl.ds(at, SLICE)], w, NT)
    cg = cg.astype(jnp.bfloat16)
    v = v_ref[...]
    q_t, k_t, cg_t = q_ref[...].T, k_ref[...].T, cg.T
    grad_scores = []
    for head in range(8):
        lanes = slice(head // 4 * SLICE, head // 4 * SLICE + SLICE)
        grad_scores.append(dot(cg[:, lanes], head_only(v[:, lanes], head % 4), NT))
    score_grads = []
    for head in range(8):
        attention = attention_ref[head]
        total = jnp.sum(attention * grad_scores[head], axis=1, keepdims=True)
        score_grad = attention * (grad_scores[head] - total) * (1.0 / math.sqrt(HEAD_DIM))
        score_grads.append(score_grad.astype(jnp.bfloat16))
    for head in range(8):
        rows = slice(head * HEAD_DIM, (head + 1) * HEAD_DIM)
        attention_b = attention_ref[head].astype(jnp.bfloat16)
        g_ref[0, rows] = dot(k_t[rows], score_grads[head], NT).astype(jnp.bfloat16)
        g_ref[1, rows] = dot(q_t[rows], score_grads[head], NN).astype(jnp.bfloat16)
        g_ref[2, rows] = dot(cg_t[rows], attention_b, NN).astype(jnp.bfloat16)


def backward_call(place, attention, moved, pieces):
    def column(base):
        return pl.BlockSpec((ROWS, 2 * SLICE), lambda i, s: (0, base + i))

    return pl.pallas_call(
        backward_kernel,
        grid_spec=pltpu.PrefetchScalarGridSpec(
            num_scalar_prefetch=1,
            grid=(2,),
            in_specs=[
                pl.BlockSpec((8, ROWS, ROWS), lambda i, s: (i, 0, 0)),
                column(0),
                column(2),
                column(4),
                pl.BlockSpec((ROWS, D), lambda i, s: (0, 3)),
            ]
            + [pl.BlockSpec((16, 16, SLICE), lambda i, s: (i, 0, 3))] * 8,
            out_specs=pl.BlockSpec((3, 2 * SLICE, ROWS), lambda i, s: (0, i, 0)),
        ),
        out_shape=jax.ShapeDtypeStruct((3, D, ROWS), jnp.bfloat16),
        compiler_params=pltpu.CompilerParams(vmem_limit_bytes=16 * 2**20),
        cost_estimate=pl.CostEstimate(
            flops=3 * 10**9, bytes_accessed=10 * 2**20, transcendentals=0
        ),
        name="attention_grads",
    )(place, attention, moved, moved, moved, moved, *pieces)


def projection_kernel(place, g_ref, *refs):
    pieces, o_ref = refs[:8], refs[8]
    x_at, core = place[0], place[1]
    width = 3 * SLICE
    total = jnp.zeros((SLICE, ROWS), jnp.float32)
    for d in range(4):
        w = weight_rows(pieces[d], pieces[4 + d], core, slice(0, width))
        at = pl.multiple_of(lax.rem(x_at + d, 4) * width, width)
        total = total + dot(w, g_ref[pl.ds(at, width)], NN)
    o_ref[...] = total.astype(jnp.bfloat16).T


def projection_call(place, grads, pieces):
    return pl.pallas_call(
        projection_kernel,
        grid_spec=pltpu.PrefetchScalarGridSpec(
            num_scalar_prefetch=1,
            grid=(4,),
            in_specs=[pl.BlockSpec((3 * D, ROWS), lambda i, s: (0, 0))]
            + [pl.BlockSpec((8, 16, D), lambda i, s: (i, 0, 0))] * 8,
            out_specs=pl.BlockSpec((ROWS, SLICE), lambda i, s: (0, i)),
        ),
        out_shape=jax.ShapeDtypeStruct((ROWS, D), jnp.bfloat16),
        compiler_params=pltpu.CompilerParams(vmem_limit_bytes=20 * 2**20),
        cost_estimate=pl.CostEstimate(
            flops=2 * 10**9, bytes_accessed=8 * 2**20, transcendentals=0
        ),
        name="input_projection",
    )(place, grads.reshape(3 * D, ROWS), *pieces)


def own_columns(input_weights, output_weight):
    x_at = lax.axis_index("x")
    mine = jnp.concatenate(
        [
            lax.dynamic_slice(input_weights, (0, x_at * 3 * SLICE), (16, 3 * SLICE)),
            lax.dynamic_slice(output_weight, (0, x_at * SLICE), (16, SLICE)),
        ],
        axis=1,
    )
    return jnp.broadcast_to(mine[None], (32, 16, D))


def swap_cores(block):
    return lax.ppermute(block, "c", ring(2, 1))


def spread_x(plane):
    half = plane.shape[0] // 2
    after = lax.ppermute(plane, "x", ring(4, -1))
    before = lax.ppermute(plane, "x", ring(4, 1))
    far_a = lax.ppermute(before[:half], "x", ring(4, 1))
    far_b = lax.ppermute(after[half:], "x", ring(4, -1))
    return [plane, after, far_a, far_b, before]


def add_kernel(a_ref, b_ref, o_ref):
    total = a_ref[...].astype(jnp.float32) + b_ref[...].astype(jnp.float32)
    o_ref[...] = total.astype(jnp.bfloat16)


def sum_cores(keep, send):
    block = pl.BlockSpec((256, D), lambda i: (i, 0))
    return pl.pallas_call(
        add_kernel,
        grid=(2,),
        in_specs=[block, block],
        out_specs=block,
        out_shape=jax.ShapeDtypeStruct(keep.shape, keep.dtype),
        compiler_params=pltpu.CompilerParams(vmem_limit_bytes=8 * 2**20),
        name="sum_cores",
    )(keep, swap_cores(send))


def shares_kernel(factor, s_ref, o_ref):
    o_ref[...] = jnp.sum(s_ref[...].astype(jnp.float32), axis=0) * factor


def sum_shares(shares, factor):
    return pl.pallas_call(
        functools.partial(shares_kernel, factor),
        grid=(2,),
        in_specs=[pl.BlockSpec((32, 16, D // 2), lambda i: (0, 0, i))],
        out_specs=pl.BlockSpec((16, D // 2), lambda i: (0, i)),
        out_shape=jax.ShapeDtypeStruct((16, D), jnp.float32),
        compiler_params=pltpu.CompilerParams(vmem_limit_bytes=8 * 2**20),
        name="sum_shares",
    )(shares)


def write_kernel(i_ref, o_ref):
    o_ref[...] = i_ref[...]


def write_out(rows):
    block = pl.BlockSpec((64, D), lambda i: (i, 0))
    return pl.pallas_call(
        write_kernel,
        grid=(4,),
        in_specs=[block],
        out_specs=block,
        out_shape=jax.ShapeDtypeStruct(rows.shape, rows.dtype),
        compiler_params=pltpu.CompilerParams(vmem_limit_bytes=8 * 2**20),
        name="write_out",
    )(rows)


def sum_x(share):
    for bit in (1, 2):
        share = share + lax.ppermute(share, "x", [(i, i ^ bit) for i in range(4)])
    return share


def on_device(query_rows, key_rows, value_rows, upstream, input_weights, output_weight):
    factor = 1.0 / (8 * math.sqrt(16384))
    place = jnp.stack([lax.axis_index(a) for a in ("x", "c")]).astype(jnp.int32)
    columns = own_columns(input_weights, output_weight)
    columns, query_rows, key_rows, value_rows, upstream = lax.optimization_barrier(
        (columns, query_rows, key_rows, value_rows, upstream)
    )
    plane = lax.all_to_all(columns, PLANE_AXES, 0, 0, tiled=True)
    sent = jnp.concatenate(
        [a.reshape(CLIP_LEN, PATCH_BLOCK, D) for a in (query_rows, key_rows, value_rows, upstream)],
        axis=2,
    )
    sent, plane = lax.optimization_barrier((sent, plane))
    moved = lax.all_to_all(sent, CLIP_AXES, 0, 0, tiled=True).reshape(ROWS, 4 * D)
    moved, own = lax.optimization_barrier((moved, spread_x(plane)))
    attention, keep, send = forward_call(place, moved)
    attention, share, own = lax.optimization_barrier((attention, sum_cores(keep, send), own))
    share = lax.all_to_all(share.reshape(32, 16, D), PLANE_AXES, 0, 0, tiled=True)
    own = [own[0], own[1], jnp.concatenate(own[2:4], axis=0), own[4]]
    pieces = own + [swap_cores(piece) for piece in own]
    grads = backward_call(place, attention, moved, pieces)
    result = projection_call(place, grads, pieces).reshape(CLIP_LEN, PATCH_BLOCK, D)
    result, share = lax.optimization_barrier((result, share))
    input_gradient = lax.all_to_all(result, CLIP_AXES, 0, 0, tiled=True)
    share = sum_x(sum_shares(share, factor))
    other = lax.ppermute(share, "zh", ring(2, 1))
    input_gradient = write_out(input_gradient.reshape(ROWS, D))
    input_gradient, other = lax.optimization_barrier((input_gradient, other))
    weight_gradient = share + other
    return (input_gradient.reshape(query_rows.shape), weight_gradient)


def solution(mesh):
    axes = ("yh", "yl", "zl", "c", "zh", "x")
    fine = Mesh(mesh.devices.reshape(2, 4, 4, 2, 2, 4), axes)
    seq, dp = ("yh", "yl", "zl", "c"), ("zh", "x")
    rows = P(dp, seq, None, None)
    return jax.shard_map(
        on_device,
        mesh=fine,
        in_specs=(rows, rows, rows, rows, P(seq, None), P(seq, None)),
        out_specs=(rows, P(seq, None)),
        check_vma=False,
    )
```
